32 devices in a mesh: dp: 4 (over x, core), fsdp: 8 (over z, y).
Axes of the slice: x: 2, y: 2, z: 4, core: 2. Of those that a mesh axis runs over, the one named last changes fastest.
Arguments:
- tokens: bfloat16 [32768, 1024], P(('dp', 'fsdp')), may hold values from -6 to 6
- first_values: bfloat16 [32768, 1024], P(('dp', 'fsdp')), may hold values from -6 to 6
- lengths: int32 [32], P(('dp', 'fsdp')), may hold values from 256 to 1024, as said below
- cotangent: bfloat16 [32768, 1024], P(('dp', 'fsdp')), may hold values from -6 to 6
- w_query: bfloat16 [1024, 1024], P('dp', 'fsdp'), may hold values from -0.1875 to 0.1875
- w_key: bfloat16 [1024, 1024], P('dp', 'fsdp'), may hold values from -0.1875 to 0.1875
- w_value: bfloat16 [1024, 1024], P('dp', 'fsdp'), may hold values from -0.1875 to 0.1875
- w_out: bfloat16 [1024, 1024], P('dp', 'fsdp'), may hold values from -0.75 to 0.75
- w_gate: bfloat16 [1024, 2816], P('dp', 'fsdp'), may hold values from -0.1875 to 0.1875
- w_up: bfloat16 [1024, 2816], P('dp', 'fsdp'), may hold values from -0.1875 to 0.1875
- w_down: bfloat16 [2816, 1024], P('dp', 'fsdp'), may hold values from -0.109375 to 0.109375
- norm_one: bfloat16 [1024], P('fsdp'), may hold values from 0.5 to 1.5
- norm_two: bfloat16 [1024], P('fsdp'), may hold values from 0.5 to 1.5
Outputs:
- layer_out: bfloat16 [32768, 1024], P(('dp', 'fsdp'))
- input_grad: float32 [32768, 1024], P(('dp', 'fsdp'))
- first_grad: float32 [32768, 1024], P(('dp', 'fsdp'))
- query_grad: float32 [1024, 1024], P('dp', 'fsdp')
- key_grad: float32 [1024, 1024], P('dp', 'fsdp')
- value_grad: float32 [1024, 1024], P('dp', 'fsdp')
- out_grad: float32 [1024, 1024], P('dp', 'fsdp')
- gate_grad: float32 [1024, 2816], P('dp', 'fsdp')
- up_grad: float32 [1024, 2816], P('dp', 'fsdp')
- down_grad: float32 [2816, 1024], P('dp', 'fsdp')
- gain_one_grad: float32 [1024], P('fsdp')
- gain_two_grad: float32 [1024], P('fsdp')
The draws below stay inside these ranges and needn't reach their ends.
Inputs may be any that keep to these rules, and one draw needn't show every extreme that they name: `lengths`: live tokens of each sequence; slots from there to 1024 are padding. At least one sequence is 1024 long.
All inputs are finite; a program needn't handle non-finite values.
Results may differ from the reference program's by a relative error of at most 0.014.
Values may be sent and summed in bfloat16 or wider, within the bound.
A program may use at most 320 MiB of HBM per device.

```python
import jax
import jax.numpy as jnp
from jax import lax

D = 1024
HEADS = 16
HEAD_DIM = 64
FF = 2816
LEN = 1024
NSEQ = 32
TOKENS = 32768


def draw_lengths(key, part):
    key = jax.random.fold_in(key, 11)
    base_key, pick_key = jax.random.split(key)
    uniform_int = jax.random.randint(base_key, (NSEQ,), 0, LEN, dtype=jnp.int32)
    drawn_len = LEN // 4 + uniform_int * uniform_int // LEN * 3 // 4
    chosen = jax.random.randint(pick_key, (), 0, NSEQ, dtype=jnp.int32)
    return jnp.where(jnp.arange(NSEQ, dtype=jnp.int32) == chosen, LEN, drawn_len).astype(jnp.int32)


def levels(stream_key, dims, cuts, low, top_value):
    loudness, own = 1.0, jax.random.fold_in(stream_key, 6)
    for dim, blocks in cuts:
        heights = jnp.exp(jax.random.uniform(jax.random.fold_in(own, dim), (blocks,), jnp.float32, low / len(cuts), top_value / len(cuts)))
        loudness = loudness * jnp.repeat(heights, dims[dim] // blocks).reshape([-1 if axis == dim else 1 for axis in range(len(dims))])
    return loudness


def gaussian(rng, dims, width, reach, cuts=(), kind=jnp.bfloat16):
    drawn = width * jax.random.normal(rng, dims, jnp.float32)
    if cuts:
        drawn = drawn * levels(rng, dims, cuts, -0.22, 0.18)
    return jnp.clip(drawn, -reach, reach).astype(kind)


def setup_inputs(seed: int = 0) -> dict:
    arg_keys = jax.random.split(jax.random.key(seed), 14)
    return {
        "tokens": gaussian(arg_keys[0], (TOKENS, D), 1.0, 6.0, ((0, 32),)),
        "first_values": gaussian(arg_keys[1], (TOKENS, D), 1.0, 6.0, ((0, 32),)),
        "lengths": draw_lengths(jax.random.fold_in(arg_keys[13], 71), 0),
        "cotangent": gaussian(arg_keys[3], (TOKENS, D), 1.0, 6.0, ((0, 32),)),
        "w_query": gaussian(arg_keys[4], (D, D), D ** -0.5, 0.1875, ((0, 4), (1, 8))),
        "w_key": gaussian(arg_keys[5], (D, D), D ** -0.5, 0.1875, ((0, 4), (1, 8))),
        "w_value": gaussian(arg_keys[6], (D, D), D ** -0.5, 0.1875, ((0, 4), (1, 8))),
        "w_out": gaussian(arg_keys[7], (D, D), (D // 16) ** -0.5, 0.75, ((0, 4), (1, 8))),
        "w_gate": gaussian(arg_keys[8], (D, FF), D ** -0.5, 0.1875, ((0, 4), (1, 8))),
        "w_up": gaussian(arg_keys[9], (D, FF), D ** -0.5, 0.1875, ((0, 4), (1, 8))),
        "w_down": gaussian(arg_keys[10], (FF, D), FF ** -0.5, 0.109375, ((0, 4), (1, 8))),
        "norm_one": jnp.clip(1.0 + 0.1 * jax.random.normal(arg_keys[11], (D,), jnp.float32), 0.5, 1.5).astype(jnp.bfloat16),
        "norm_two": jnp.clip(1.0 + 0.1 * jax.random.normal(arg_keys[12], (D,), jnp.float32), 0.5, 1.5).astype(jnp.bfloat16),
    }


@jax.custom_vjp
def low(v):
    return lax.optimization_barrier(v.astype(jnp.bfloat16)).astype(jnp.float32)

@jax.custom_vjp
def low_back(v):
    return v

def low_keep(v):
    return (low(v), None)

def low_pass(kept, grad):
    return (grad,)

def back_keep(v):
    return (v, None)

def back_low(kept, grad):
    return (low(grad),)
low.defvjp(low_keep, low_pass)
low_back.defvjp(back_keep, back_low)
highest = lax.Precision.HIGHEST

def matmul(left_side, right_side):
    return jnp.dot(left_side, right_side, precision=highest)

def rms_norm(values, gain_vec):
    inverse = lax.rsqrt(lax.optimization_barrier(jnp.mean(values * values, axis=-1, keepdims=True)) + 1e-06)
    return values * inverse * gain_vec

def rotate(values, positions):
    half_dim = values.shape[-1] // 2
    frequency = 10000.0 ** (-jnp.arange(half_dim, dtype=jnp.float32) * 2.0 / values.shape[-1])
    angles = positions[:, None].astype(jnp.float32) * frequency[None, :]
    cosine = jnp.cos(angles)[:, None, :]
    sine_table = jnp.sin(angles)[:, None, :]
    first_half = values[..., :half_dim]
    second_half = values[..., half_dim:]
    return jnp.concatenate([first_half * cosine - second_half * sine_table, second_half * cosine + first_half * sine_table], axis=-1)

def layer(tokens, first_values, w_query, w_key, w_value, w_out, w_gate, w_up, w_down, gain_one, gain_two, keep_rows, positions):
    normed = low(rms_norm(tokens, gain_one))
    query_rot = low(rotate(low_back(matmul(normed, w_query)).reshape(-1, HEADS, HEAD_DIM), positions))
    key_rot = low(rotate(low_back(matmul(normed, w_key)).reshape(-1, HEADS, HEAD_DIM), positions))
    values_mix = low(0.5 * low_back(matmul(normed, w_value)) + 0.5 * first_values).reshape(-1, HEADS, HEAD_DIM)
    scores = low_back(jnp.einsum('qhd,khd->hqk', query_rot, key_rot, precision=highest)) * 0.125
    allowed = positions[None, :] <= positions[:, None]
    scores = jnp.where(allowed[None], scores, -1000000000.0)
    weights = low(jax.nn.softmax(scores, axis=-1))
    attended = jnp.einsum('hqk,khd->qhd', weights, values_mix, precision=highest)
    attended = low(low_back(attended)).reshape(-1, HEADS * HEAD_DIM)
    mixed_rows = tokens + low_back(matmul(attended, w_out))
    second = low(rms_norm(mixed_rows, gain_two))
    gate_val = low_back(matmul(second, w_gate))
    up_val = low_back(matmul(second, w_up))
    hidden = low(jax.nn.silu(gate_val) * up_val)
    return keep_rows[:, None] * (mixed_rows + low_back(matmul(hidden, w_down)))

def reference(tokens, first_values, lengths, cotangent, w_query, w_key, w_value, w_out, w_gate, w_up, w_down, norm_one, norm_two):
    params = tuple((matrix.astype(jnp.float32) for matrix in (w_query, w_key, w_value, w_out, w_gate, w_up, w_down, norm_one, norm_two)))
    seq_count = TOKENS // LEN
    positions = jnp.arange(LEN, dtype=jnp.int32)

    def one_sequence(totals, pieces):
        seq_tokens, seq_first, seq_length, seq_cot = pieces
        keep_rows = (positions < seq_length).astype(jnp.float32)

        def forward(tok_rows, first_rows, *weights):
            return layer(tok_rows, first_rows, *weights, keep_rows, positions)
        output, pullback = jax.vjp(forward, seq_tokens.astype(jnp.float32), seq_first.astype(jnp.float32), *params)
        gradients = pullback(seq_cot.astype(jnp.float32))
        totals = tuple((acc + new for acc, new in zip(totals, gradients[2:])))
        return (totals, (output.astype(jnp.bfloat16), gradients[0], gradients[1]))
    initial = tuple((jnp.zeros_like(matrix) for matrix in params))
    totals, stacked = lax.scan(one_sequence, initial, (tokens.reshape(seq_count, LEN, D), first_values.reshape(seq_count, LEN, D), lengths, cotangent.reshape(seq_count, LEN, D)))
    outputs, token_grads, first_grads = stacked
    return (outputs.reshape(TOKENS, D), token_grads.reshape(TOKENS, D), first_grads.reshape(TOKENS, D), totals[0], totals[1], totals[2], totals[3], totals[4], totals[5], totals[6], totals[7], totals[8])
```

```python
from functools import partial

import jax
import jax.numpy as jnp
import numpy as np
from jax import lax
from jax.experimental import pallas as pl
from jax.experimental.pallas import tpu as pltpu
from jax.sharding import PartitionSpec as P

HEADS = 16
HEAD_DIM = 64


def rms_norm(values, gain_vec):
    inverse = lax.rsqrt(jnp.mean(values * values, axis=-1, keepdims=True) + 1e-06)
    return values * inverse * gain_vec


def rotate(values, positions):
    half_dim = values.shape[-1] // 2
    frequency = 10000.0 ** (-jnp.arange(half_dim, dtype=jnp.float32) * 2.0 / values.shape[-1])
    angles = positions[:, None].astype(jnp.float32) * frequency[None, :]
    cosine = jnp.cos(angles)[:, None, :]
    sine_table = jnp.sin(angles)[:, None, :]
    first_half = values[..., :half_dim]
    second_half = values[..., half_dim:]
    return jnp.concatenate(
        [
            first_half * cosine - second_half * sine_table,
            second_half * cosine + first_half * sine_table,
        ],
        axis=-1,
    )


def masked_scores(query_blk, keys_seq, row_start, block_rows):
    scores = (
        jnp.einsum("qhd,khd->hqk", query_blk, keys_seq, preferred_element_type=jnp.float32) * 0.125
    )
    key_pos = jnp.arange(keys_seq.shape[0], dtype=jnp.int32)
    query_pos = row_start + jnp.arange(block_rows, dtype=jnp.int32)
    allowed = key_pos[None, :] <= query_pos[:, None]
    return jnp.where(allowed[None], scores, -1000000000.0)


def attend_forward(query_seq, keys_seq, values_seq, block_rows):
    block_count = query_seq.shape[0] // block_rows

    def one_block(block_index):
        row_start = block_index * block_rows
        query_blk = lax.dynamic_slice_in_dim(query_seq, row_start, block_rows, 0)
        scores = masked_scores(query_blk, keys_seq, row_start, block_rows)
        row_peak = jnp.max(scores, axis=-1, keepdims=True)
        exponent = jnp.exp(scores - row_peak)
        row_total = jnp.sum(exponent, axis=-1, keepdims=True)
        prob_low = (exponent / row_total).astype(jnp.bfloat16)
        attended = jnp.einsum(
            "hqk,khd->qhd", prob_low, values_seq, preferred_element_type=jnp.float32
        )
        return (attended, (row_peak + jnp.log(row_total))[..., 0])

    attended, logsum = lax.map(one_block, jnp.arange(block_count, dtype=jnp.int32))
    return (attended.reshape(query_seq.shape), logsum)


def attend_backward(query_seq, keys_seq, values_seq, grad_seq, logsum, block_rows):
    block_count = query_seq.shape[0] // block_rows

    def one_block(running, block_index):
        key_acc, value_acc = running
        row_start = block_index * block_rows
        query_blk = lax.dynamic_slice_in_dim(query_seq, row_start, block_rows, 0)
        grad_blk = lax.dynamic_slice_in_dim(grad_seq, row_start, block_rows, 0)
        scores = masked_scores(query_blk, keys_seq, row_start, block_rows)
        prob_wide = jnp.exp(scores - logsum[block_index][..., None])
        prob_low = prob_wide.astype(jnp.bfloat16)
        grad_probs = jnp.einsum(
            "qhd,khd->hqk", grad_blk, values_seq, preferred_element_type=jnp.float32
        )
        row_delta = jnp.sum(prob_wide * grad_probs, axis=-1, keepdims=True)
        grad_scores = (0.125 * (prob_wide * (grad_probs - row_delta))).astype(jnp.bfloat16)
        query_part = jnp.einsum(
            "hqk,khd->qhd", grad_scores, keys_seq, preferred_element_type=jnp.float32
        )
        key_acc = key_acc + jnp.einsum(
            "hqk,qhd->khd", grad_scores, query_blk, preferred_element_type=jnp.float32
        )
        value_acc = value_acc + jnp.einsum(
            "hqk,qhd->khd", prob_low, grad_blk, preferred_element_type=jnp.float32
        )
        return ((key_acc, value_acc), query_part)

    zeros_seq = jnp.zeros(query_seq.shape, jnp.float32)
    (key_acc, value_acc), query_parts = lax.scan(
        one_block, (zeros_seq, zeros_seq), jnp.arange(block_count, dtype=jnp.int32)
    )
    return (query_parts.reshape(query_seq.shape), key_acc, value_acc)


def on_device_general(
    tokens,
    first_values,
    lengths,
    cotangent,
    w_query,
    w_key,
    w_value,
    w_out,
    w_gate,
    w_up,
    w_down,
    norm_one,
    norm_two,
):
    (
        query_part,
        key_part,
        value_part,
        out_part,
        gate_part,
        up_part,
        down_part,
        gain_first,
        gain_second,
    ) = (
        lax.all_gather(w_query, "fsdp", axis=1, tiled=True),
        lax.all_gather(w_key, "fsdp", axis=1, tiled=True),
        lax.all_gather(w_value, "fsdp", axis=1, tiled=True),
        lax.all_gather(w_out, "fsdp", axis=1, tiled=True),
        lax.all_gather(w_gate, "fsdp", axis=1, tiled=True),
        lax.all_gather(w_up, "fsdp", axis=1, tiled=True),
        lax.all_gather(w_down, "fsdp", axis=1, tiled=True),
        lax.all_gather(norm_one, "fsdp", axis=0, tiled=True),
        lax.all_gather(norm_two, "fsdp", axis=0, tiled=True),
    )
    query_full, key_full, value_full, out_full, gate_full, up_full, down_full = (
        lax.all_gather(query_part, "dp", axis=0, tiled=True),
        lax.all_gather(key_part, "dp", axis=0, tiled=True),
        lax.all_gather(value_part, "dp", axis=0, tiled=True),
        lax.all_gather(out_part, "dp", axis=0, tiled=True),
        lax.all_gather(gate_part, "dp", axis=0, tiled=True),
        lax.all_gather(up_part, "dp", axis=0, tiled=True),
        lax.all_gather(down_part, "dp", axis=0, tiled=True),
    )
    gathered = (
        query_full,
        key_full,
        value_full,
        out_full,
        gate_full,
        up_full,
        down_full,
        gain_first,
        gain_second,
    )
    query_w, key_w, value_w, out_w, gate_w, up_w, down_w, gain_first, gain_second = gathered
    gain_one_wide = gain_first.astype(jnp.float32)
    gain_two_wide = gain_second.astype(jnp.float32)
    tok_rows = tokens.shape[0]
    seq_count = lengths.shape[0]
    seq_len = tok_rows // seq_count
    block_rows = min(512, seq_len)
    positions = jnp.arange(seq_len, dtype=jnp.int32)
    row_positions = jnp.tile(positions, seq_count)
    keep_rows = (positions[None, :] < lengths[:, None]).astype(jnp.float32).reshape(tok_rows, 1)

    def by_sequence(array):
        return array.reshape(seq_count, seq_len, HEADS, HEAD_DIM)

    tokens_wide = tokens.astype(jnp.float32)
    normed_low = rms_norm(tokens_wide, gain_one_wide).astype(jnp.bfloat16)
    query_lin = jnp.dot(normed_low, query_w, preferred_element_type=jnp.float32).reshape(
        tok_rows, HEADS, HEAD_DIM
    )
    key_lin = jnp.dot(normed_low, key_w, preferred_element_type=jnp.float32).reshape(
        tok_rows, HEADS, HEAD_DIM
    )
    value_lin = jnp.dot(normed_low, value_w, preferred_element_type=jnp.float32)
    rope_rows = partial(rotate, positions=row_positions)
    query_rot = rope_rows(query_lin).astype(jnp.bfloat16)
    key_rot = rope_rows(key_lin).astype(jnp.bfloat16)
    values_mix = (0.5 * value_lin + 0.5 * first_values.astype(jnp.float32)).astype(jnp.bfloat16)
    attended, logsum = lax.map(
        lambda pieces: attend_forward(pieces[0], pieces[1], pieces[2], block_rows),
        (by_sequence(query_rot), by_sequence(key_rot), by_sequence(values_mix)),
    )
    attended_low = attended.reshape(tok_rows, HEADS * HEAD_DIM).astype(jnp.bfloat16)
    mixed_rows = tokens_wide + jnp.dot(attended_low, out_w, preferred_element_type=jnp.float32)
    second_low = rms_norm(mixed_rows, gain_two_wide).astype(jnp.bfloat16)
    gate_val = jnp.dot(second_low, gate_w, preferred_element_type=jnp.float32)
    up_val = jnp.dot(second_low, up_w, preferred_element_type=jnp.float32)
    hidden = (jax.nn.silu(gate_val) * up_val).astype(jnp.bfloat16)
    ffn_out = jnp.dot(hidden, down_w, preferred_element_type=jnp.float32)
    layer_out = (keep_rows * (mixed_rows + ffn_out)).astype(jnp.bfloat16)
    (
        query_part,
        key_part,
        value_part,
        out_part,
        gate_part,
        up_part,
        down_part,
        gain_first,
        gain_second,
    ) = (
        lax.all_gather(w_query, "fsdp", axis=1, tiled=True),
        lax.all_gather(w_key, "fsdp", axis=1, tiled=True),
        lax.all_gather(w_value, "fsdp", axis=1, tiled=True),
        lax.all_gather(w_out, "fsdp", axis=1, tiled=True),
        lax.all_gather(w_gate, "fsdp", axis=1, tiled=True),
        lax.all_gather(w_up, "fsdp", axis=1, tiled=True),
        lax.all_gather(w_down, "fsdp", axis=1, tiled=True),
        lax.all_gather(norm_one, "fsdp", axis=0, tiled=True),
        lax.all_gather(norm_two, "fsdp", axis=0, tiled=True),
    )
    query_w, key_w, value_w, out_w, gate_w, up_w, down_w = (
        lax.all_gather(query_part, "dp", axis=0, tiled=True),
        lax.all_gather(key_part, "dp", axis=0, tiled=True),
        lax.all_gather(value_part, "dp", axis=0, tiled=True),
        lax.all_gather(out_part, "dp", axis=0, tiled=True),
        lax.all_gather(gate_part, "dp", axis=0, tiled=True),
        lax.all_gather(up_part, "dp", axis=0, tiled=True),
        lax.all_gather(down_part, "dp", axis=0, tiled=True),
    )
    gain_one_wide = gain_first.astype(jnp.float32)
    gain_two_wide = gain_second.astype(jnp.float32)
    grad_top = cotangent.astype(jnp.float32) * keep_rows
    grad_ffn = grad_top.astype(jnp.bfloat16)
    down_sum = jnp.einsum("rf,rd->fd", hidden, grad_ffn, preferred_element_type=jnp.float32)
    grad_hidden = jnp.einsum("rd,fd->rf", grad_ffn, down_w, preferred_element_type=jnp.float32)
    _, swiglu_back = jax.vjp(lambda gate_in, up_in: jax.nn.silu(gate_in) * up_in, gate_val, up_val)
    grad_gate, grad_up = swiglu_back(grad_hidden)
    grad_gate_low = grad_gate.astype(jnp.bfloat16)
    grad_up_low = grad_up.astype(jnp.bfloat16)
    gate_sum = jnp.einsum(
        "rd,rf->df", second_low, grad_gate_low, preferred_element_type=jnp.float32
    )
    up_sum = jnp.einsum("rd,rf->df", second_low, grad_up_low, preferred_element_type=jnp.float32)
    grad_second = jnp.einsum(
        "rf,df->rd", grad_gate_low, gate_w, preferred_element_type=jnp.float32
    ) + jnp.einsum("rf,df->rd", grad_up_low, up_w, preferred_element_type=jnp.float32)
    _, norm_two_back = jax.vjp(rms_norm, mixed_rows, gain_two_wide)
    grad_mixed_norm, gain_two_sum = norm_two_back(grad_second)
    grad_mixed = grad_top + grad_mixed_norm
    grad_branch = grad_mixed.astype(jnp.bfloat16)
    out_sum = jnp.einsum("rd,re->de", attended_low, grad_branch, preferred_element_type=jnp.float32)
    grad_attended = jnp.einsum(
        "re,de->rd", grad_branch, out_w, preferred_element_type=jnp.float32
    ).astype(jnp.bfloat16)
    query_back, key_back, value_back = lax.map(
        lambda pieces: attend_backward(
            pieces[0], pieces[1], pieces[2], pieces[3], pieces[4], block_rows
        ),
        (
            by_sequence(query_rot),
            by_sequence(key_rot),
            by_sequence(values_mix),
            by_sequence(grad_attended),
            logsum,
        ),
    )
    _, rope_back = jax.vjp(rope_rows, query_lin)
    grad_query_low = (
        rope_back(query_back.reshape(tok_rows, HEADS, HEAD_DIM))[0]
        .reshape(tok_rows, HEADS * HEAD_DIM)
        .astype(jnp.bfloat16)
    )
    grad_key_low = (
        rope_back(key_back.reshape(tok_rows, HEADS, HEAD_DIM))[0]
        .reshape(tok_rows, HEADS * HEAD_DIM)
        .astype(jnp.bfloat16)
    )
    value_mix_grad = value_back.reshape(tok_rows, HEADS * HEAD_DIM)
    first_grad = 0.5 * value_mix_grad
    grad_value_low = (0.5 * value_mix_grad).astype(jnp.bfloat16)
    query_sum = jnp.einsum(
        "rd,re->de", normed_low, grad_query_low, preferred_element_type=jnp.float32
    )
    key_sum = jnp.einsum("rd,re->de", normed_low, grad_key_low, preferred_element_type=jnp.float32)
    value_sum = jnp.einsum(
        "rd,re->de", normed_low, grad_value_low, preferred_element_type=jnp.float32
    )
    grad_normed = (
        jnp.einsum("re,de->rd", grad_query_low, query_w, preferred_element_type=jnp.float32)
        + jnp.einsum("re,de->rd", grad_key_low, key_w, preferred_element_type=jnp.float32)
        + jnp.einsum("re,de->rd", grad_value_low, value_w, preferred_element_type=jnp.float32)
    )
    _, norm_one_back = jax.vjp(rms_norm, tokens_wide, gain_one_wide)
    grad_tokens_norm, gain_one_sum = norm_one_back(grad_normed)
    input_grad = grad_mixed + grad_tokens_norm
    (
        query_red,
        key_red,
        value_red,
        out_red,
        gate_red,
        up_red,
        down_red,
        gain_one_red,
        gain_two_red,
    ) = (
        lax.psum_scatter(query_sum, "fsdp", scatter_dimension=1, tiled=True),
        lax.psum_scatter(key_sum, "fsdp", scatter_dimension=1, tiled=True),
        lax.psum_scatter(value_sum, "fsdp", scatter_dimension=1, tiled=True),
        lax.psum_scatter(out_sum, "fsdp", scatter_dimension=1, tiled=True),
        lax.psum_scatter(gate_sum, "fsdp", scatter_dimension=1, tiled=True),
        lax.psum_scatter(up_sum, "fsdp", scatter_dimension=1, tiled=True),
        lax.psum_scatter(down_sum, "fsdp", scatter_dimension=1, tiled=True),
        lax.psum_scatter(gain_one_sum, "fsdp", scatter_dimension=0, tiled=True),
        lax.psum_scatter(gain_two_sum, "fsdp", scatter_dimension=0, tiled=True),
    )
    query_grad, key_grad, value_grad, out_grad, gate_grad, up_grad, down_grad = (
        lax.psum_scatter(query_red, "dp", scatter_dimension=0, tiled=True),
        lax.psum_scatter(key_red, "dp", scatter_dimension=0, tiled=True),
        lax.psum_scatter(value_red, "dp", scatter_dimension=0, tiled=True),
        lax.psum_scatter(out_red, "dp", scatter_dimension=0, tiled=True),
        lax.psum_scatter(gate_red, "dp", scatter_dimension=0, tiled=True),
        lax.psum_scatter(up_red, "dp", scatter_dimension=0, tiled=True),
        lax.psum_scatter(down_red, "dp", scatter_dimension=0, tiled=True),
    )
    gain_one_grad, gain_two_grad = lax.psum((gain_one_red, gain_two_red), "dp")
    return (
        layer_out,
        input_grad,
        first_grad,
        query_grad,
        key_grad,
        value_grad,
        out_grad,
        gate_grad,
        up_grad,
        down_grad,
        gain_one_grad,
        gain_two_grad,
    )


MESH_ID = pl.DeviceIdType.MESH
BF = jnp.bfloat16
F32 = jnp.float32
NN = (((1,), (0,)), ((), ()))
NT = (((1,), (1,)), ((), ()))
TN = (((0,), (0,)), ((), ()))


def mm(a, b, dims):
    return lax.dot_general(a, b, dims, preferred_element_type=F32)


def place():
    dp, fs = lax.axis_index("dp"), lax.axis_index("fsdp")
    return dp // 2, dp % 2, fs // 2, fs % 2


def device(x, c, z, y):
    return (2 * x + c, 2 * z + y)


def greet(x, c, z, y):
    barrier = pltpu.get_barrier_semaphore()
    peers = [device(1 - x, c, z, y), device(x, 1 - c, z, y), device(x, c, z, 1 - y)]
    peers += [device(x, c, lax.rem(z + d, 4), y) for d in (1, 2, 3)]
    for peer in peers:
        pl.semaphore_signal(barrier, inc=1, device_id=peer, device_id_type=MESH_ID)
    pl.semaphore_wait(barrier, len(peers))


def block(spec, ref, z, y, x, c, half):
    rows, cols, along = spec
    size = rows if half is None else rows // 2
    start = 0 if half is None else half * (rows // 2)
    dp = 2 * x + c
    if along == "rows":
        return ref.at[z, y, pl.ds(pl.multiple_of(dp * rows + start, 16), size)]
    return ref.at[z, y, pl.ds(start, size), pl.ds(pl.multiple_of(dp * cols, 128), cols)]


ALL = slice(None)


class Gather:
    def __init__(self, at, spec, shard, full, send, recv, local, index):
        self.at, self.spec, self.shard, self.full = at, spec, shard, full
        self.send, self.recv, self.local, self.index = send, recv, local, index
        self.copies = {}

    def part(self, z, y, x, c, half):
        return block(self.spec, self.full, z, y, x, c, half)

    def start(self, slot, source, target, peer):
        copy = pltpu.make_async_remote_copy(
            src_ref=source,
            dst_ref=target,
            send_sem=self.send.at[self.index, slot],
            recv_sem=self.recv.at[self.index, slot],
            device_id=peer,
            device_id_type=MESH_ID,
        )
        copy.start()
        self.copies[slot] = copy

    def go(self, slot, region, peer):
        self.start(slot, region, region, peer)

    def arrive(self, *slots):
        for slot in slots:
            self.copies[slot].wait_recv()

    def tick0(self):
        x, c, z, y = self.at
        own = self.part(z, y, x, c, None)
        for d in (1, 2, 3):
            self.start(d - 1, self.shard, own, device(x, c, lax.rem(z + d, 4), y))
        self.own = pltpu.make_async_copy(self.shard, own, self.local.at[self.index])
        self.own.start()

    def tick1(self):
        x, c, z, y = self.at
        self.own.wait()
        self.arrive(0, 1, 2)
        self.go(4, self.part(ALL, y, x, c, 0), device(1 - x, c, z, y))
        self.go(5, self.part(ALL, y, x, c, 1), device(x, c, z, 1 - y))
        self.go(3, self.part(ALL, y, x, c, None), device(x, 1 - c, z, y))

    def tick2(self):
        x, c, z, y = self.at
        across, beside, other = device(1 - x, c, z, y), device(x, c, z, 1 - y), device(x, 1 - c, z, y)
        self.arrive(4, 5)
        self.go(6, self.part(ALL, y, 0, c, 0), beside)
        self.go(7, self.part(ALL, y, 1, c, 0), beside)
        self.go(8, self.part(ALL, ALL, x, c, 1), across)
        self.go(9, self.part(ALL, y, 1 - x, c, 0), other)
        self.go(10, self.part(ALL, 1 - y, x, c, 1), other)

    def tick3(self):
        x, c, z, y = self.at
        other = device(x, 1 - c, z, y)
        self.arrive(6, 7, 8)
        self.go(11, self.part(ALL, 1 - y, 0, c, 0), other)
        self.go(12, self.part(ALL, 1 - y, 1, c, 0), other)
        self.go(13, self.part(ALL, ALL, 1 - x, c, 1), other)

    def tick4(self):
        self.arrive(3, 9, 10, 11, 12, 13)

    def finish(self):
        for copy in self.copies.values():
            copy.wait_send()


QKV, OUT, GATE, UP, DOWN, GAIN = range(6)
SPECS = {
    QKV: (256, 384, "rows"),
    OUT: (256, 128, "rows"),
    GATE: (352, 256, "cols"),
    UP: (352, 256, "cols"),
    DOWN: (704, 128, "rows"),
    GAIN: (32, 128, "rows"),
}


def full_shape(spec):
    rows, cols, along = spec
    return (4, 2, 4 * rows, cols) if along == "rows" else (4, 2, rows, 4 * cols)


def turn(u, cosine, low_sine, high_sine):
    return u * cosine + pltpu.roll(u, 96, 1) * low_sine + pltpu.roll(u, 32, 1) * high_sine


def head_mask(shape, head):
    lane = lax.broadcasted_iota(jnp.int32, shape, 1)
    return (lane < 64) if head == 0 else (lane >= 64)


def attend_pair(q, k, v, blk):
    rows = q.shape[0]
    v_turned = v.T
    out, sums = [], [[], []]
    key_index = lax.broadcasted_iota(jnp.int32, (blk, blk), 0)
    query_index = lax.broadcasted_iota(jnp.int32, (blk, blk), 1)
    allowed = key_index <= query_index
    for j in range(rows // blk):
        lo, hi = j * blk, (j + 1) * blk
        parts = []
        for head in range(2):
            qh = jnp.where(head_mask((blk, 128), head), q[lo:hi], 0)
            s = mm(k[:hi], qh, NT)
            tail = jnp.where(allowed, s[lo:hi], -1000000000.0)
            peak = jnp.max(tail, axis=0, keepdims=True)
            if j:
                peak = jnp.maximum(peak, jnp.max(s[:lo], axis=0, keepdims=True))
            e = jnp.exp(tail - peak)
            total = jnp.sum(e, axis=0, keepdims=True)
            e = e.astype(BF)
            if j:
                head_part = jnp.exp(s[:lo] - peak)
                total = total + jnp.sum(head_part, axis=0, keepdims=True)
                e = jnp.concatenate([head_part.astype(BF), e], axis=0)
            parts.append(mm(v_turned[head * 64 : head * 64 + 64, :hi], e, NN) * (1.0 / total))
            sums[head].append(peak + jnp.log(total))
        out.append(jnp.concatenate(parts, axis=0).T.astype(BF))
    return jnp.concatenate(out, axis=0), [jnp.concatenate(s, axis=1) for s in sums]


def forward_kernel(
    length, tokens, first, s_qkv, s_out, s_gate, s_up, s_down, s_gain, cosine, low_sine, high_sine,
    layer_out, n1_o, q_o, k_o, v_o, o_o, lse_o, x2_o, n2_o, h_o, a_o, b_o, g_qkv, g_out, g_gate, g_up, g_down, g_gain,
    f_qkv, f_out, f_gate, f_up, f_down, f_gain,
    tok, fst, n1, q, k, v, o, lse, x2, n2, h, ab, cos, sin_lo, sin_hi,
    send, recv, local, fetch, store, store_ab,
):
    at = place()
    tok_copy = pltpu.make_async_copy(tokens, tok, fetch.at[0])
    tok_copy.start()
    greet(*at)
    shards = {QKV: s_qkv, OUT: s_out, GATE: s_gate, UP: s_up, DOWN: s_down, GAIN: s_gain}
    fulls = {QKV: f_qkv, OUT: f_out, GATE: f_gate, UP: f_up, DOWN: f_down, GAIN: f_gain}
    outs = {QKV: g_qkv, OUT: g_out, GATE: g_gate, UP: g_up, DOWN: g_down, GAIN: g_gain}
    ag = {g: Gather(at, SPECS[g], shards[g], fulls[g], send, recv, local, g) for g in SPECS}
    for g in (GAIN, QKV, OUT, GATE, UP, DOWN):
        ag[g].tick0()
    loads = [
        pltpu.make_async_copy(a, b, fetch.at[i + 1])
        for i, (a, b) in enumerate(((first, fst), (cosine, cos), (low_sine, sin_lo), (high_sine, sin_hi)))
    ]
    for copy in loads:
        copy.start()
    stores = []

    def save(a, b):
        copy = pltpu.make_async_copy(a, b, store.at[len(stores)])
        copy.start()
        stores.append(copy)

    tok_copy.wait()
    ag[GAIN].tick1()
    ag[GAIN].tick2()
    ag[QKV].tick1()
    ag[GAIN].tick3()
    ag[GAIN].tick4()
    gain = jnp.concatenate([f_gain[z, y, 0:32, :] for z in range(4) for y in range(2)], axis=1).astype(F32)
    gain_one, gain_two = gain[0:1], gain[16:17]
    rows = tok.shape[0]
    step = 256

    def norm_one(i, _):
        at_rows = pl.ds(pl.multiple_of(i * step, step), step)
        t = tok[at_rows].astype(F32)
        inverse = lax.rsqrt(jnp.mean(t * t, axis=-1, keepdims=True) + 1e-06)
        n1[at_rows] = (t * inverse * gain_one).astype(BF)
        return 0

    lax.fori_loop(0, rows // step, norm_one, 0)
    save(n1, n1_o)
    ag[QKV].tick2()
    ag[OUT].tick1()
    ag[QKV].tick3()
    ag[OUT].tick2()
    ag[GATE].tick1()
    ag[QKV].tick4()
    save(f_qkv, g_qkv)
    save(f_gain, g_gain)
    for copy in loads:
        copy.wait()

    def project(z, _):
        weights = jnp.concatenate([f_qkv[z, 0], f_qkv[z, 1]], axis=1)
        for part in range(2):
            at_rows = pl.ds(part * (rows // 2), rows // 2)
            both = mm(n1[at_rows], weights, NN)
            for y in range(2):
                one = both[:, y * 384 : y * 384 + 384]
                c, lo, hi = cos[at_rows], sin_lo[at_rows], sin_hi[at_rows]
                q[2 * z + y, at_rows] = (turn(one[:, 0:128], c, lo, hi).astype(BF).astype(F32) * 0.125).astype(BF)
                k[2 * z + y, at_rows] = turn(one[:, 128:256], c, lo, hi).astype(BF)
                cols = pl.ds(pl.multiple_of((2 * z + y) * 128, 128), 128)
                v[2 * z + y, at_rows] = (0.5 * one[:, 256:384] + 0.5 * fst[at_rows, cols].astype(F32)).astype(BF)
        return 0

    def attend(p, _):
        result, sums = attend_pair(q[p], k[p], v[p], min(256, rows))
        o[:, pl.ds(pl.multiple_of(p * 128, 128), 128)] = result
        for head in range(2):
            lse[p, pl.ds(head, 1)] = sums[head]
        return 0

    lax.fori_loop(0, 2, project, 0)
    ag[OUT].tick3()
    lax.fori_loop(2, 4, project, 0)
    save(q, q_o)
    save(k, k_o)
    save(v, v_o)
    ag[GATE].tick2()
    ag[UP].tick1()
    lax.fori_loop(0, 4, attend, 0)
    ag[OUT].tick4()
    save(f_out, g_out)
    ag[GATE].tick3()
    ag[UP].tick2()
    ag[DOWN].tick1()
    lax.fori_loop(4, 8, attend, 0)
    save(o, o_o)
    save(lse, lse_o)

    def mix(z, _):
        weights = jnp.concatenate([f_out[z, 0], f_out[z, 1]], axis=1)
        cols = pl.ds(pl.multiple_of(z * 256, 256), 256)
        x2[:, cols] = tok[:, cols].astype(F32) + mm(o[...], weights, NN)
        return 0

    lax.fori_loop(0, 4, mix, 0)
    save(x2, x2_o)

    def norm_two(i, _):
        at_rows = pl.ds(pl.multiple_of(i * step, step), step)
        t = x2[at_rows]
        inverse = lax.rsqrt(jnp.mean(t * t, axis=-1, keepdims=True) + 1e-06)
        n2[at_rows] = (t * inverse * gain_two).astype(BF)
        return 0

    lax.fori_loop(0, rows // step, norm_two, 0)
    save(n2, n2_o)
    ag[GATE].tick4()
    save(f_gate, g_gate)
    ag[UP].tick3()
    ag[DOWN].tick2()
    ag[UP].tick4()
    save(f_up, g_up)
    width = 352

    def put_ab(f, slot):
        at_h = pl.ds(pl.multiple_of(f * width, 16), width)
        return [
            pltpu.make_async_copy(ab.at[slot, i], target.at[at_h], store_ab.at[slot, i])
            for i, target in enumerate((a_o, b_o))
        ]

    def hidden(f, _):
        z, y = f // 2, f % 2
        slot = lax.rem(f, 2)

        @pl.when(f >= 2)
        def _():
            for copy in put_ab(f - 2, slot):
                copy.wait()

        for part in range(2):
            span = pl.ds(part * 176, 176)
            gate = mm(f_gate[z, y, span], n2[...], NT)
            up = mm(f_up[z, y, span], n2[...], NT)
            s = 1.0 / (1.0 + jnp.exp(-gate))
            silu = gate * s
            at_h = pl.ds(pl.multiple_of(f * width + part * 176, 16), 176)
            h[at_h] = (silu * up).astype(BF)
            ab[slot, 0, span] = (up * (s * (1.0 + gate * (1.0 - s)))).astype(BF)
            ab[slot, 1, span] = silu.astype(BF)
        for copy in put_ab(f, slot):
            copy.start()
        return 0

    lax.fori_loop(0, 4, hidden, 0)
    ag[DOWN].tick3()
    lax.fori_loop(4, 8, hidden, 0)
    save(h, h_o)
    ag[DOWN].tick4()
    save(f_down, g_down)
    live = length[0]

    def last(z, _):
        weights = jnp.concatenate([f_down[z, 0], f_down[z, 1]], axis=1)
        cols = pl.ds(pl.multiple_of(z * 256, 256), 256)
        result = x2[:, cols] + mm(h[...], weights, TN)
        keep = lax.broadcasted_iota(jnp.int32, (rows, 256), 0) < live
        fst[:, cols] = jnp.where(keep, result, 0.0).astype(BF)
        return 0

    lax.fori_loop(0, 4, last, 0)
    save(fst, layer_out)
    for g in SPECS:
        ag[g].finish()
    for copy in stores:
        copy.wait()
    for f in (6, 7):
        for copy in put_ab(f, f % 2):
            copy.wait()


def forward(length, tokens, first, shards, tables):
    rows, width = tokens.shape
    hidden = 8 * shards[GATE].shape[0]
    order = (QKV, OUT, GATE, UP, DOWN, GAIN)
    half = jax.ShapeDtypeStruct((rows, width), BF)
    pairs = jax.ShapeDtypeStruct((8, rows, 128), BF)
    tall = jax.ShapeDtypeStruct((hidden, rows), BF)
    logs = jax.ShapeDtypeStruct((8, 2, rows), F32)
    wide = jax.ShapeDtypeStruct((rows, width), F32)
    fulls = [jax.ShapeDtypeStruct(full_shape(SPECS[g]), BF) for g in order]
    outs = [half, half, pairs, pairs, pairs, half, logs, wide, half, tall, tall, tall] + fulls
    anywhere = pl.BlockSpec(memory_space=pl.ANY)
    scratch = [pltpu.VMEM(s.shape, s.dtype) for s in fulls]
    scratch += [pltpu.VMEM(s.shape, s.dtype) for s in (half, half, half, pairs, pairs, pairs, half, logs, wide, half, tall)]
    scratch += [pltpu.VMEM((2, 2, hidden // 8, rows), BF)]
    scratch += [pltpu.VMEM((rows, 128), F32)] * 3
    scratch += [
        pltpu.SemaphoreType.DMA((6, 14)),
        pltpu.SemaphoreType.DMA((6, 14)),
        pltpu.SemaphoreType.DMA((6,)),
        pltpu.SemaphoreType.DMA((5,)),
        pltpu.SemaphoreType.DMA((len(outs),)),
        pltpu.SemaphoreType.DMA((2, 2)),
    ]
    return pl.pallas_call(
        forward_kernel,
        out_shape=outs,
        in_specs=[pl.BlockSpec(memory_space=pltpu.SMEM)] + [anywhere] * 11,
        out_specs=[anywhere] * len(outs),
        scratch_shapes=scratch,
        compiler_params=pltpu.CompilerParams(
            collective_id=0, has_side_effects=True, vmem_limit_bytes=63 << 20
        ),
        name="forward",
    )(length, tokens, first, *[shards[g] for g in order], *tables)


def rope_tables(rows):
    position = np.arange(rows, dtype=np.float32)[:, None]
    frequency = np.float32(10000.0) ** (-np.arange(32, dtype=np.float32) * np.float32(2.0) / np.float32(64))
    angle = (position * frequency[None, :]).astype(np.float32)
    cosine, sine, zero = np.cos(angle), np.sin(angle), np.zeros_like(angle)
    join = lambda parts: np.concatenate(parts, axis=1).astype(np.float32)
    return join([cosine] * 4), join([-sine, zero] * 2), join([zero, sine] * 2)


def on_slice(
    tokens, first_values, lengths, cotangent, w_query, w_key, w_value, w_out, w_gate, w_up, w_down, norm_one, norm_two,
):
    rows, width = tokens.shape
    gains = jnp.concatenate([jnp.broadcast_to(g[None], (16, 128)) for g in (norm_one, norm_two)], axis=0)
    shards = {
        QKV: jnp.concatenate([w_query, w_key, w_value], axis=1),
        OUT: w_out,
        GATE: w_gate.T,
        UP: w_up.T,
        DOWN: w_down,
        GAIN: gains,
    }
    tables = [jnp.asarray(t) for t in rope_tables(rows)]
    (
        layer_out, n1, q, k, v, o, lse, x2, n2, h, a, b, g_qkv, g_out, g_gate, g_up, g_down, g_gain,
    ) = forward(lengths, tokens, first_values, shards, tables)
    g_qkv = g_qkv.reshape(8, 1024, 384)
    whole = lambda w: jnp.moveaxis(w, 0, 1).reshape(w.shape[1], -1)
    query_w, key_w, value_w = (whole(g_qkv[:, :, i * 128 : i * 128 + 128]) for i in range(3))
    out_w, down_w = whole(g_out.reshape(8, 1024, 128)), whole(g_down.reshape(8, 2816, 128))
    gate_t, up_t = g_gate.reshape(2816, 1024), g_up.reshape(2816, 1024)
    gain_one_wide = g_gain.reshape(8, 128, 128)[:, 0].reshape(-1).astype(jnp.float32)
    gain_two_wide = g_gain.reshape(8, 128, 128)[:, 16].reshape(-1).astype(jnp.float32)
    positions = jnp.arange(rows, dtype=jnp.int32)
    keep_rows = (positions[None, :] < lengths[:, None]).astype(jnp.float32).reshape(rows, 1)
    heads = lambda t: jnp.moveaxis(t, 0, 1).reshape(rows, HEADS, HEAD_DIM)
    query_rot, key_rot, values_mix = heads(q * 8), heads(k), heads(v)
    logsum = jnp.moveaxis(lse.reshape(16, 2, 512), 1, 0)
    tokens_wide = tokens.astype(jnp.float32)
    grad_top = cotangent.astype(jnp.float32) * keep_rows
    grad_ffn = grad_top.astype(jnp.bfloat16)
    down_sum = jnp.einsum("fr,rd->fd", h, grad_ffn, preferred_element_type=jnp.float32)
    grad_hidden = jnp.einsum("rd,fd->fr", grad_ffn, down_w, preferred_element_type=jnp.float32)
    grad_gate_low = (grad_hidden * a).astype(jnp.bfloat16)
    grad_up_low = (grad_hidden * b).astype(jnp.bfloat16)
    gate_sum = jnp.einsum("rd,fr->df", n2, grad_gate_low, preferred_element_type=jnp.float32)
    up_sum = jnp.einsum("rd,fr->df", n2, grad_up_low, preferred_element_type=jnp.float32)
    grad_second = jnp.einsum("fr,fd->rd", grad_gate_low, gate_t, preferred_element_type=jnp.float32) + jnp.einsum(
        "fr,fd->rd", grad_up_low, up_t, preferred_element_type=jnp.float32
    )
    _, norm_two_back = jax.vjp(rms_norm, x2, gain_two_wide)
    grad_mixed_norm, gain_two_sum = norm_two_back(grad_second)
    grad_mixed = grad_top + grad_mixed_norm
    grad_branch = grad_mixed.astype(jnp.bfloat16)
    out_sum = jnp.einsum("rd,re->de", o, grad_branch, preferred_element_type=jnp.float32)
    grad_attended = jnp.einsum("re,de->rd", grad_branch, out_w, preferred_element_type=jnp.float32).astype(jnp.bfloat16)
    query_back, key_back, value_back = attend_backward(
        query_rot, key_rot, values_mix, grad_attended.reshape(rows, HEADS, HEAD_DIM), logsum, 512
    )
    rope_rows = partial(rotate, positions=positions)
    _, rope_back = jax.vjp(rope_rows, query_back)
    grad_query_low = rope_back(query_back)[0].reshape(rows, 1024).astype(jnp.bfloat16)
    grad_key_low = rope_back(key_back)[0].reshape(rows, 1024).astype(jnp.bfloat16)
    value_mix_grad = value_back.reshape(rows, 1024)
    first_grad = 0.5 * value_mix_grad
    grad_value_low = (0.5 * value_mix_grad).astype(jnp.bfloat16)
    dot = lambda e, s, t: jnp.einsum(e, s, t, preferred_element_type=jnp.float32)
    query_sum, key_sum, value_sum = (dot("rd,re->de", n1, g) for g in (grad_query_low, grad_key_low, grad_value_low))
    grad_normed = (
        dot("re,de->rd", grad_query_low, query_w)
        + dot("re,de->rd", grad_key_low, key_w)
        + dot("re,de->rd", grad_value_low, value_w)
    )
    _, norm_one_back = jax.vjp(rms_norm, tokens_wide, gain_one_wide)
    grad_tokens_norm, gain_one_sum = norm_one_back(grad_normed)
    input_grad = grad_mixed + grad_tokens_norm

    def reduce(total):
        total = lax.psum_scatter(total, "dp", scatter_dimension=0, tiled=True)
        return lax.psum_scatter(total, "fsdp", scatter_dimension=1, tiled=True)

    sums = (query_sum, key_sum, value_sum, out_sum, gate_sum, up_sum, down_sum)
    sums = [reduce(s) for s in sums]
    gain_grads = lax.psum(
        [lax.psum_scatter(g, "fsdp", scatter_dimension=0, tiled=True) for g in (gain_one_sum, gain_two_sum)], "dp"
    )
    return (layer_out, input_grad, first_grad, *sums, *gain_grads)


def solution(mesh):
    in_specs = (
        P(("dp", "fsdp"), None),
        P(("dp", "fsdp"), None),
        P(("dp", "fsdp")),
        P(("dp", "fsdp"), None),
        P("dp", "fsdp"),
        P("dp", "fsdp"),
        P("dp", "fsdp"),
        P("dp", "fsdp"),
        P("dp", "fsdp"),
        P("dp", "fsdp"),
        P("dp", "fsdp"),
        P("fsdp"),
        P("fsdp"),
    )
    out_specs = (
        P(("dp", "fsdp"), None),
        P(("dp", "fsdp"), None),
        P(("dp", "fsdp"), None),
        P("dp", "fsdp"),
        P("dp", "fsdp"),
        P("dp", "fsdp"),
        P("dp", "fsdp"),
        P("dp", "fsdp"),
        P("dp", "fsdp"),
        P("dp", "fsdp"),
        P("fsdp"),
        P("fsdp"),
    )
    on_device = on_slice if dict(mesh.shape) == {"dp": 4, "fsdp": 8} else on_device_general
    return jax.shard_map(
        on_device, mesh=mesh, in_specs=in_specs, out_specs=out_specs, check_vma=False
    )
```

```python
from functools import partial

import jax
import jax.numpy as jnp
import numpy as np
from jax import lax
from jax.experimental import pallas as pl
from jax.experimental.pallas import tpu as pltpu
from jax.sharding import PartitionSpec as P

HEADS = 16
HEAD_DIM = 64


def rms_norm(values, gain_vec):
    inverse = lax.rsqrt(jnp.mean(values * values, axis=-1, keepdims=True) + 1e-06)
    return values * inverse * gain_vec


def rotate(values, positions):
    half_dim = values.shape[-1] // 2
    frequency = 10000.0 ** (-jnp.arange(half_dim, dtype=jnp.float32) * 2.0 / values.shape[-1])
    angles = positions[:, None].astype(jnp.float32) * frequency[None, :]
    cosine = jnp.cos(angles)[:, None, :]
    sine_table = jnp.sin(angles)[:, None, :]
    first_half = values[..., :half_dim]
    second_half = values[..., half_dim:]
    return jnp.concatenate(
        [
            first_half * cosine - second_half * sine_table,
            second_half * cosine + first_half * sine_table,
        ],
        axis=-1,
    )


def masked_scores(query_blk, keys_seq, row_start, block_rows):
    scores = (
        jnp.einsum("qhd,khd->hqk", query_blk, keys_seq, preferred_element_type=jnp.float32) * 0.125
    )
    key_pos = jnp.arange(keys_seq.shape[0], dtype=jnp.int32)
    query_pos = row_start + jnp.arange(block_rows, dtype=jnp.int32)
    allowed = key_pos[None, :] <= query_pos[:, None]
    return jnp.where(allowed[None], scores, -1000000000.0)


def attend_forward(query_seq, keys_seq, values_seq, block_rows):
    block_count = query_seq.shape[0] // block_rows

    def one_block(block_index):
        row_start = block_index * block_rows
        query_blk = lax.dynamic_slice_in_dim(query_seq, row_start, block_rows, 0)
        scores = masked_scores(query_blk, keys_seq, row_start, block_rows)
        row_peak = jnp.max(scores, axis=-1, keepdims=True)
        exponent = jnp.exp(scores - row_peak)
        row_total = jnp.sum(exponent, axis=-1, keepdims=True)
        prob_low = (exponent / row_total).astype(jnp.bfloat16)
        attended = jnp.einsum(
            "hqk,khd->qhd", prob_low, values_seq, preferred_element_type=jnp.float32
        )
        return (attended, (row_peak + jnp.log(row_total))[..., 0])

    attended, logsum = lax.map(one_block, jnp.arange(block_count, dtype=jnp.int32))
    return (attended.reshape(query_seq.shape), logsum)


def attend_backward(query_seq, keys_seq, values_seq, grad_seq, logsum, block_rows):
    block_count = query_seq.shape[0] // block_rows

    def one_block(running, block_index):
        key_acc, value_acc = running
        row_start = block_index * block_rows
        query_blk = lax.dynamic_slice_in_dim(query_seq, row_start, block_rows, 0)
        grad_blk = lax.dynamic_slice_in_dim(grad_seq, row_start, block_rows, 0)
        scores = masked_scores(query_blk, keys_seq, row_start, block_rows)
        prob_wide = jnp.exp(scores - logsum[block_index][..., None])
        prob_low = prob_wide.astype(jnp.bfloat16)
        grad_probs = jnp.einsum(
            "qhd,khd->hqk", grad_blk, values_seq, preferred_element_type=jnp.float32
        )
        row_delta = jnp.sum(prob_wide * grad_probs, axis=-1, keepdims=True)
        grad_scores = (0.125 * (prob_wide * (grad_probs - row_delta))).astype(jnp.bfloat16)
        query_part = jnp.einsum(
            "hqk,khd->qhd", grad_scores, keys_seq, preferred_element_type=jnp.float32
        )
        key_acc = key_acc + jnp.einsum(
            "hqk,qhd->khd", grad_scores, query_blk, preferred_element_type=jnp.float32
        )
        value_acc = value_acc + jnp.einsum(
            "hqk,qhd->khd", prob_low, grad_blk, preferred_element_type=jnp.float32
        )
        return ((key_acc, value_acc), query_part)

    zeros_seq = jnp.zeros(query_seq.shape, jnp.float32)
    (key_acc, value_acc), query_parts = lax.scan(
        one_block, (zeros_seq, zeros_seq), jnp.arange(block_count, dtype=jnp.int32)
    )
    return (query_parts.reshape(query_seq.shape), key_acc, value_acc)


def on_device_general(
    tokens,
    first_values,
    lengths,
    cotangent,
    w_query,
    w_key,
    w_value,
    w_out,
    w_gate,
    w_up,
    w_down,
    norm_one,
    norm_two,
):
    (
        query_part,
        key_part,
        value_part,
        out_part,
        gate_part,
        up_part,
        down_part,
        gain_first,
        gain_second,
    ) = (
        lax.all_gather(w_query, "fsdp", axis=1, tiled=True),
        lax.all_gather(w_key, "fsdp", axis=1, tiled=True),
        lax.all_gather(w_value, "fsdp", axis=1, tiled=True),
        lax.all_gather(w_out, "fsdp", axis=1, tiled=True),
        lax.all_gather(w_gate, "fsdp", axis=1, tiled=True),
        lax.all_gather(w_up, "fsdp", axis=1, tiled=True),
        lax.all_gather(w_down, "fsdp", axis=1, tiled=True),
        lax.all_gather(norm_one, "fsdp", axis=0, tiled=True),
        lax.all_gather(norm_two, "fsdp", axis=0, tiled=True),
    )
    query_full, key_full, value_full, out_full, gate_full, up_full, down_full = (
        lax.all_gather(query_part, "dp", axis=0, tiled=True),
        lax.all_gather(key_part, "dp", axis=0, tiled=True),
        lax.all_gather(value_part, "dp", axis=0, tiled=True),
        lax.all_gather(out_part, "dp", axis=0, tiled=True),
        lax.all_gather(gate_part, "dp", axis=0, tiled=True),
        lax.all_gather(up_part, "dp", axis=0, tiled=True),
        lax.all_gather(down_part, "dp", axis=0, tiled=True),
    )
    gathered = (
        query_full,
        key_full,
        value_full,
        out_full,
        gate_full,
        up_full,
        down_full,
        gain_first,
        gain_second,
    )
    query_w, key_w, value_w, out_w, gate_w, up_w, down_w, gain_first, gain_second = gathered
    gain_one_wide = gain_first.astype(jnp.float32)
    gain_two_wide = gain_second.astype(jnp.float32)
    tok_rows = tokens.shape[0]
    seq_count = lengths.shape[0]
    seq_len = tok_rows // seq_count
    block_rows = min(512, seq_len)
    positions = jnp.arange(seq_len, dtype=jnp.int32)
    row_positions = jnp.tile(positions, seq_count)
    keep_rows = (positions[None, :] < lengths[:, None]).astype(jnp.float32).reshape(tok_rows, 1)

    def by_sequence(array):
        return array.reshape(seq_count, seq_len, HEADS, HEAD_DIM)

    tokens_wide = tokens.astype(jnp.float32)
    normed_low = rms_norm(tokens_wide, gain_one_wide).astype(jnp.bfloat16)
    query_lin = jnp.dot(normed_low, query_w, preferred_element_type=jnp.float32).reshape(
        tok_rows, HEADS, HEAD_DIM
    )
    key_lin = jnp.dot(normed_low, key_w, preferred_element_type=jnp.float32).reshape(
        tok_rows, HEADS, HEAD_DIM
    )
    value_lin = jnp.dot(normed_low, value_w, preferred_element_type=jnp.float32)
    rope_rows = partial(rotate, positions=row_positions)
    query_rot = rope_rows(query_lin).astype(jnp.bfloat16)
    key_rot = rope_rows(key_lin).astype(jnp.bfloat16)
    values_mix = (0.5 * value_lin + 0.5 * first_values.astype(jnp.float32)).astype(jnp.bfloat16)
    attended, logsum = lax.map(
        lambda pieces: attend_forward(pieces[0], pieces[1], pieces[2], block_rows),
        (by_sequence(query_rot), by_sequence(key_rot), by_sequence(values_mix)),
    )
    attended_low = attended.reshape(tok_rows, HEADS * HEAD_DIM).astype(jnp.bfloat16)
    mixed_rows = tokens_wide + jnp.dot(attended_low, out_w, preferred_element_type=jnp.float32)
    second_low = rms_norm(mixed_rows, gain_two_wide).astype(jnp.bfloat16)
    gate_val = jnp.dot(second_low, gate_w, preferred_element_type=jnp.float32)
    up_val = jnp.dot(second_low, up_w, preferred_element_type=jnp.float32)
    hidden = (jax.nn.silu(gate_val) * up_val).astype(jnp.bfloat16)
    ffn_out = jnp.dot(hidden, down_w, preferred_element_type=jnp.float32)
    layer_out = (keep_rows * (mixed_rows + ffn_out)).astype(jnp.bfloat16)
    (
        query_part,
        key_part,
        value_part,
        out_part,
        gate_part,
        up_part,
        down_part,
        gain_first,
        gain_second,
    ) = (
        lax.all_gather(w_query, "fsdp", axis=1, tiled=True),
        lax.all_gather(w_key, "fsdp", axis=1, tiled=True),
        lax.all_gather(w_value, "fsdp", axis=1, tiled=True),
        lax.all_gather(w_out, "fsdp", axis=1, tiled=True),
        lax.all_gather(w_gate, "fsdp", axis=1, tiled=True),
        lax.all_gather(w_up, "fsdp", axis=1, tiled=True),
        lax.all_gather(w_down, "fsdp", axis=1, tiled=True),
        lax.all_gather(norm_one, "fsdp", axis=0, tiled=True),
        lax.all_gather(norm_two, "fsdp", axis=0, tiled=True),
    )
    query_w, key_w, value_w, out_w, gate_w, up_w, down_w = (
        lax.all_gather(query_part, "dp", axis=0, tiled=True),
        lax.all_gather(key_part, "dp", axis=0, tiled=True),
        lax.all_gather(value_part, "dp", axis=0, tiled=True),
        lax.all_gather(out_part, "dp", axis=0, tiled=True),
        lax.all_gather(gate_part, "dp", axis=0, tiled=True),
        lax.all_gather(up_part, "dp", axis=0, tiled=True),
        lax.all_gather(down_part, "dp", axis=0, tiled=True),
    )
    gain_one_wide = gain_first.astype(jnp.float32)
    gain_two_wide = gain_second.astype(jnp.float32)
    grad_top = cotangent.astype(jnp.float32) * keep_rows
    grad_ffn = grad_top.astype(jnp.bfloat16)
    down_sum = jnp.einsum("rf,rd->fd", hidden, grad_ffn, preferred_element_type=jnp.float32)
    grad_hidden = jnp.einsum("rd,fd->rf", grad_ffn, down_w, preferred_element_type=jnp.float32)
    _, swiglu_back = jax.vjp(lambda gate_in, up_in: jax.nn.silu(gate_in) * up_in, gate_val, up_val)
    grad_gate, grad_up = swiglu_back(grad_hidden)
    grad_gate_low = grad_gate.astype(jnp.bfloat16)
    grad_up_low = grad_up.astype(jnp.bfloat16)
    gate_sum = jnp.einsum(
        "rd,rf->df", second_low, grad_gate_low, preferred_element_type=jnp.float32
    )
    up_sum = jnp.einsum("rd,rf->df", second_low, grad_up_low, preferred_element_type=jnp.float32)
    grad_second = jnp.einsum(
        "rf,df->rd", grad_gate_low, gate_w, preferred_element_type=jnp.float32
    ) + jnp.einsum("rf,df->rd", grad_up_low, up_w, preferred_element_type=jnp.float32)
    _, norm_two_back = jax.vjp(rms_norm, mixed_rows, gain_two_wide)
    grad_mixed_norm, gain_two_sum = norm_two_back(grad_second)
    grad_mixed = grad_top + grad_mixed_norm
    grad_branch = grad_mixed.astype(jnp.bfloat16)
    out_sum = jnp.einsum("rd,re->de", attended_low, grad_branch, preferred_element_type=jnp.float32)
    grad_attended = jnp.einsum(
        "re,de->rd", grad_branch, out_w, preferred_element_type=jnp.float32
    ).astype(jnp.bfloat16)
    query_back, key_back, value_back = lax.map(
        lambda pieces: attend_backward(
            pieces[0], pieces[1], pieces[2], pieces[3], pieces[4], block_rows
        ),
        (
            by_sequence(query_rot),
            by_sequence(key_rot),
            by_sequence(values_mix),
            by_sequence(grad_attended),
            logsum,
        ),
    )
    _, rope_back = jax.vjp(rope_rows, query_lin)
    grad_query_low = (
        rope_back(query_back.reshape(tok_rows, HEADS, HEAD_DIM))[0]
        .reshape(tok_rows, HEADS * HEAD_DIM)
        .astype(jnp.bfloat16)
    )
    grad_key_low = (
        rope_back(key_back.reshape(tok_rows, HEADS, HEAD_DIM))[0]
        .reshape(tok_rows, HEADS * HEAD_DIM)
        .astype(jnp.bfloat16)
    )
    value_mix_grad = value_back.reshape(tok_rows, HEADS * HEAD_DIM)
    first_grad = 0.5 * value_mix_grad
    grad_value_low = (0.5 * value_mix_grad).astype(jnp.bfloat16)
    query_sum = jnp.einsum(
        "rd,re->de", normed_low, grad_query_low, preferred_element_type=jnp.float32
    )
    key_sum = jnp.einsum("rd,re->de", normed_low, grad_key_low, preferred_element_type=jnp.float32)
    value_sum = jnp.einsum(
        "rd,re->de", normed_low, grad_value_low, preferred_element_type=jnp.float32
    )
    grad_normed = (
        jnp.einsum("re,de->rd", grad_query_low, query_w, preferred_element_type=jnp.float32)
        + jnp.einsum("re,de->rd", grad_key_low, key_w, preferred_element_type=jnp.float32)
        + jnp.einsum("re,de->rd", grad_value_low, value_w, preferred_element_type=jnp.float32)
    )
    _, norm_one_back = jax.vjp(rms_norm, tokens_wide, gain_one_wide)
    grad_tokens_norm, gain_one_sum = norm_one_back(grad_normed)
    input_grad = grad_mixed + grad_tokens_norm
    (
        query_red,
        key_red,
        value_red,
        out_red,
        gate_red,
        up_red,
        down_red,
        gain_one_red,
        gain_two_red,
    ) = (
        lax.psum_scatter(query_sum, "fsdp", scatter_dimension=1, tiled=True),
        lax.psum_scatter(key_sum, "fsdp", scatter_dimension=1, tiled=True),
        lax.psum_scatter(value_sum, "fsdp", scatter_dimension=1, tiled=True),
        lax.psum_scatter(out_sum, "fsdp", scatter_dimension=1, tiled=True),
        lax.psum_scatter(gate_sum, "fsdp", scatter_dimension=1, tiled=True),
        lax.psum_scatter(up_sum, "fsdp", scatter_dimension=1, tiled=True),
        lax.psum_scatter(down_sum, "fsdp", scatter_dimension=1, tiled=True),
        lax.psum_scatter(gain_one_sum, "fsdp", scatter_dimension=0, tiled=True),
        lax.psum_scatter(gain_two_sum, "fsdp", scatter_dimension=0, tiled=True),
    )
    query_grad, key_grad, value_grad, out_grad, gate_grad, up_grad, down_grad = (
        lax.psum_scatter(query_red, "dp", scatter_dimension=0, tiled=True),
        lax.psum_scatter(key_red, "dp", scatter_dimension=0, tiled=True),
        lax.psum_scatter(value_red, "dp", scatter_dimension=0, tiled=True),
        lax.psum_scatter(out_red, "dp", scatter_dimension=0, tiled=True),
        lax.psum_scatter(gate_red, "dp", scatter_dimension=0, tiled=True),
        lax.psum_scatter(up_red, "dp", scatter_dimension=0, tiled=True),
        lax.psum_scatter(down_red, "dp", scatter_dimension=0, tiled=True),
    )
    gain_one_grad, gain_two_grad = lax.psum((gain_one_red, gain_two_red), "dp")
    return (
        layer_out,
        input_grad,
        first_grad,
        query_grad,
        key_grad,
        value_grad,
        out_grad,
        gate_grad,
        up_grad,
        down_grad,
        gain_one_grad,
        gain_two_grad,
    )


MESH_ID = pl.DeviceIdType.MESH
BF = jnp.bfloat16
F32 = jnp.float32
NN = (((1,), (0,)), ((), ()))
NT = (((1,), (1,)), ((), ()))
TN = (((0,), (0,)), ((), ()))


def mm(a, b, dims):
    return lax.dot_general(a, b, dims, preferred_element_type=F32)


def place():
    dp, fs = lax.axis_index("dp"), lax.axis_index("fsdp")
    return dp // 2, dp % 2, fs // 2, fs % 2


def device(x, c, z, y):
    return (2 * x + c, 2 * z + y)


def greet(x, c, z, y):
    barrier = pltpu.get_barrier_semaphore()
    peers = [device(1 - x, c, z, y), device(x, 1 - c, z, y), device(x, c, z, 1 - y)]
    peers += [device(x, c, lax.rem(z + d, 4), y) for d in (1, 2, 3)]
    for peer in peers:
        pl.semaphore_signal(barrier, inc=1, device_id=peer, device_id_type=MESH_ID)
    pl.semaphore_wait(barrier, len(peers))


def block(spec, ref, z, y, x, c, half):
    rows, cols, along = spec
    size = rows if half is None else rows // 2
    start = 0 if half is None else half * (rows // 2)
    dp = 2 * x + c
    if along == "rows":
        return ref.at[z, y, pl.ds(pl.multiple_of(dp * rows + start, 16), size)]
    return ref.at[z, y, pl.ds(start, size), pl.ds(pl.multiple_of(dp * cols, 128), cols)]


ALL = slice(None)


class Gather:
    def __init__(self, at, spec, shard, full, send, recv, local, index):
        self.at, self.spec, self.shard, self.full = at, spec, shard, full
        self.send, self.recv, self.local, self.index = send, recv, local, index
        self.copies = {}

    def part(self, z, y, x, c, half):
        return block(self.spec, self.full, z, y, x, c, half)

    def start(self, slot, source, target, peer):
        copy = pltpu.make_async_remote_copy(
            src_ref=source,
            dst_ref=target,
            send_sem=self.send.at[self.index, slot],
            recv_sem=self.recv.at[self.index, slot],
            device_id=peer,
            device_id_type=MESH_ID,
        )
        copy.start()
        self.copies[slot] = copy

    def go(self, slot, region, peer):
        self.start(slot, region, region, peer)

    def arrive(self, *slots):
        for slot in slots:
            self.copies[slot].wait_recv()

    def tick0(self):
        x, c, z, y = self.at
        own = self.part(z, y, x, c, None)
        for d in (1, 2, 3):
            self.start(d - 1, self.shard, own, device(x, c, lax.rem(z + d, 4), y))
        self.own = pltpu.make_async_copy(self.shard, own, self.local.at[self.index])
        self.own.start()

    def tick1(self):
        x, c, z, y = self.at
        self.own.wait()
        self.arrive(0, 1, 2)
        self.go(4, self.part(ALL, y, x, c, 0), device(1 - x, c, z, y))
        self.go(5, self.part(ALL, y, x, c, 1), device(x, c, z, 1 - y))
        self.go(3, self.part(ALL, y, x, c, None), device(x, 1 - c, z, y))

    def tick2(self):
        x, c, z, y = self.at
        across, beside, other = device(1 - x, c, z, y), device(x, c, z, 1 - y), device(x, 1 - c, z, y)
        self.arrive(4, 5)
        self.go(6, self.part(ALL, y, 0, c, 0), beside)
        self.go(7, self.part(ALL, y, 1, c, 0), beside)
        self.go(8, self.part(ALL, ALL, x, c, 1), across)
        self.go(9, self.part(ALL, y, 1 - x, c, 0), other)
        self.go(10, self.part(ALL, 1 - y, x, c, 1), other)

    def tick3(self):
        x, c, z, y = self.at
        other = device(x, 1 - c, z, y)
        self.arrive(6, 7, 8)
        self.go(11, self.part(ALL, 1 - y, 0, c, 0), other)
        self.go(12, self.part(ALL, 1 - y, 1, c, 0), other)
        self.go(13, self.part(ALL, ALL, 1 - x, c, 1), other)

    def tick4(self):
        self.arrive(3, 9, 10, 11, 12, 13)

    def finish(self):
        for copy in self.copies.values():
            copy.wait_send()


QKV, OUT, GATE, UP, DOWN, GAIN = range(6)
SPECS = {
    QKV: (256, 384, "rows"),
    OUT: (256, 128, "rows"),
    GATE: (352, 256, "cols"),
    UP: (352, 256, "cols"),
    DOWN: (704, 128, "rows"),
    GAIN: (32, 128, "rows"),
}


def full_shape(spec):
    rows, cols, along = spec
    return (4, 2, 4 * rows, cols) if along == "rows" else (4, 2, rows, 4 * cols)


def turn(u, cosine, low_sine, high_sine):
    return u * cosine + pltpu.roll(u, 96, 1) * low_sine + pltpu.roll(u, 32, 1) * high_sine


def head_mask(shape, head):
    lane = lax.broadcasted_iota(jnp.int32, shape, 1)
    return (lane < 64) if head == 0 else (lane >= 64)


def attend_pair(q, k, v, blk):
    rows = q.shape[0]
    v_turned = v.T
    out, sums = [], [[], []]
    key_index = lax.broadcasted_iota(jnp.int32, (blk, blk), 0)
    query_index = lax.broadcasted_iota(jnp.int32, (blk, blk), 1)
    allowed = key_index <= query_index
    for j in range(rows // blk):
        lo, hi = j * blk, (j + 1) * blk
        parts = []
        for head in range(2):
            qh = jnp.where(head_mask((blk, 128), head), q[lo:hi], 0)
            s = mm(k[:hi], qh, NT)
            tail = jnp.where(allowed, s[lo:hi], -1000000000.0)
            peak = jnp.max(tail, axis=0, keepdims=True)
            if j:
                peak = jnp.maximum(peak, jnp.max(s[:lo], axis=0, keepdims=True))
            e = jnp.exp(tail - peak)
            total = jnp.sum(e, axis=0, keepdims=True)
            e = e.astype(BF)
            if j:
                head_part = jnp.exp(s[:lo] - peak)
                total = total + jnp.sum(head_part, axis=0, keepdims=True)
                e = jnp.concatenate([head_part.astype(BF), e], axis=0)
            parts.append(mm(v_turned[head * 64 : head * 64 + 64, :hi], e, NN) * (1.0 / total))
            sums[head].append(peak + jnp.log(total))
        out.append(jnp.concatenate(parts, axis=0).T.astype(BF))
    return jnp.concatenate(out, axis=0), [jnp.concatenate(s, axis=1) for s in sums]


def forward_kernel(
    length, tokens, first, s_qkv, s_out, s_gate, s_up, s_down, s_gain, cosine, low_sine, high_sine,
    layer_out, n1_o, q_o, k_o, v_o, o_o, lse_o, x2_o, n2_o, h_o, a_o, b_o, g_qkv, g_out, g_gate, g_up, g_down, g_gain,
    f_qkv, f_out, f_gate, f_up, f_down, f_gain,
    tok, fst, n1, q, k, v, o, lse, x2, n2, h, ab, cos, sin_lo, sin_hi,
    send, recv, local, fetch, store, store_ab,
):
    at = place()
    tok_copy = pltpu.make_async_copy(tokens, tok, fetch.at[0])
    tok_copy.start()
    greet(*at)
    shards = {QKV: s_qkv, OUT: s_out, GATE: s_gate, UP: s_up, DOWN: s_down, GAIN: s_gain}
    fulls = {QKV: f_qkv, OUT: f_out, GATE: f_gate, UP: f_up, DOWN: f_down, GAIN: f_gain}
    outs = {QKV: g_qkv, OUT: g_out, GATE: g_gate, UP: g_up, DOWN: g_down, GAIN: g_gain}
    ag = {g: Gather(at, SPECS[g], shards[g], fulls[g], send, recv, local, g) for g in SPECS}
    for g in (GAIN, QKV, OUT, GATE, UP, DOWN):
        ag[g].tick0()
    loads = [
        pltpu.make_async_copy(a, b, fetch.at[i + 1])
        for i, (a, b) in enumerate(((first, fst), (cosine, cos), (low_sine, sin_lo), (high_sine, sin_hi)))
    ]
    for copy in loads:
        copy.start()
    stores = []

    def save(a, b):
        copy = pltpu.make_async_copy(a, b, store.at[len(stores)])
        copy.start()
        stores.append(copy)

    tok_copy.wait()
    ag[GAIN].tick1()
    ag[GAIN].tick2()
    ag[QKV].tick1()
    ag[GAIN].tick3()
    ag[GAIN].tick4()
    gain = jnp.concatenate([f_gain[z, y, 0:32, :] for z in range(4) for y in range(2)], axis=1).astype(F32)
    gain_one, gain_two = gain[0:1], gain[16:17]
    rows = tok.shape[0]
    step = 256

    def norm_one(i, _):
        at_rows = pl.ds(pl.multiple_of(i * step, step), step)
        t = tok[at_rows].astype(F32)
        inverse = lax.rsqrt(jnp.mean(t * t, axis=-1, keepdims=True) + 1e-06)
        n1[at_rows] = (t * inverse * gain_one).astype(BF)
        return 0

    lax.fori_loop(0, rows // step, norm_one, 0)
    save(n1, n1_o)
    ag[QKV].tick2()
    ag[OUT].tick1()
    ag[QKV].tick3()
    ag[OUT].tick2()
    ag[GATE].tick1()
    ag[QKV].tick4()
    save(f_qkv, g_qkv)
    save(f_gain, g_gain)
    for copy in loads:
        copy.wait()

    def project(z, _):
        weights = jnp.concatenate([f_qkv[z, 0], f_qkv[z, 1]], axis=1)
        for part in range(2):
            at_rows = pl.ds(part * (rows // 2), rows // 2)
            both = mm(n1[at_rows], weights, NN)
            for y in range(2):
                one = both[:, y * 384 : y * 384 + 384]
                c, lo, hi = cos[at_rows], sin_lo[at_rows], sin_hi[at_rows]
                cols = pl.ds(pl.multiple_of((2 * z + y) * 128, 128), 128)
                q[at_rows, cols] = (turn(one[:, 0:128], c, lo, hi).astype(BF).astype(F32) * 0.125).astype(BF)
                k[at_rows, cols] = turn(one[:, 128:256], c, lo, hi).astype(BF)
                v[at_rows, cols] = (0.5 * one[:, 256:384] + 0.5 * fst[at_rows, cols].astype(F32)).astype(BF)
        return 0

    def attend(p, _):
        cols = pl.ds(pl.multiple_of(p * 128, 128), 128)
        result, sums = attend_pair(q[:, cols], k[:, cols], v[:, cols], min(256, rows))
        o[:, cols] = result
        for head in range(2):
            lse[p, pl.ds(head, 1)] = sums[head]
        return 0

    lax.fori_loop(0, 2, project, 0)
    ag[OUT].tick3()
    lax.fori_loop(2, 4, project, 0)
    save(q, q_o)
    save(k, k_o)
    save(v, v_o)
    ag[GATE].tick2()
    ag[UP].tick1()
    lax.fori_loop(0, 4, attend, 0)
    ag[OUT].tick4()
    save(f_out, g_out)
    ag[GATE].tick3()
    ag[UP].tick2()
    ag[DOWN].tick1()
    lax.fori_loop(4, 8, attend, 0)
    save(o, o_o)
    save(lse, lse_o)

    def mix(z, _):
        weights = jnp.concatenate([f_out[z, 0], f_out[z, 1]], axis=1)
        cols = pl.ds(pl.multiple_of(z * 256, 256), 256)
        x2[:, cols] = tok[:, cols].astype(F32) + mm(o[...], weights, NN)
        return 0

    lax.fori_loop(0, 4, mix, 0)
    save(x2, x2_o)

    def norm_two(i, _):
        at_rows = pl.ds(pl.multiple_of(i * step, step), step)
        t = x2[at_rows]
        inverse = lax.rsqrt(jnp.mean(t * t, axis=-1, keepdims=True) + 1e-06)
        n2[at_rows] = (t * inverse * gain_two).astype(BF)
        return 0

    lax.fori_loop(0, rows // step, norm_two, 0)
    save(n2, n2_o)
    ag[GATE].tick4()
    save(f_gate, g_gate)
    ag[UP].tick3()
    ag[DOWN].tick2()
    ag[UP].tick4()
    save(f_up, g_up)
    width = 352

    def put_ab(f, slot):
        at_h = pl.ds(pl.multiple_of(f * width, 16), width)
        return [
            pltpu.make_async_copy(ab.at[slot, i], target.at[at_h], store_ab.at[slot, i])
            for i, target in enumerate((a_o, b_o))
        ]

    def hidden(f, _):
        z, y = f // 2, f % 2
        slot = lax.rem(f, 2)

        @pl.when(f >= 2)
        def _():
            for copy in put_ab(f - 2, slot):
                copy.wait()

        for part in range(2):
            span = pl.ds(part * 176, 176)
            gate = mm(f_gate[z, y, span], n2[...], NT)
            up = mm(f_up[z, y, span], n2[...], NT)
            s = 1.0 / (1.0 + jnp.exp(-gate))
            silu = gate * s
            at_h = pl.ds(pl.multiple_of(f * width + part * 176, 16), 176)
            h[at_h] = (silu * up).astype(BF)
            ab[slot, 0, span] = (up * (s * (1.0 + gate * (1.0 - s)))).astype(BF)
            ab[slot, 1, span] = silu.astype(BF)
        for copy in put_ab(f, slot):
            copy.start()
        return 0

    lax.fori_loop(0, 4, hidden, 0)
    ag[DOWN].tick3()
    lax.fori_loop(4, 8, hidden, 0)
    save(h, h_o)
    ag[DOWN].tick4()
    save(f_down, g_down)
    live = length[0]

    def last(z, _):
        weights = jnp.concatenate([f_down[z, 0], f_down[z, 1]], axis=1)
        cols = pl.ds(pl.multiple_of(z * 256, 256), 256)
        result = x2[:, cols] + mm(h[...], weights, TN)
        keep = lax.broadcasted_iota(jnp.int32, (rows, 256), 0) < live
        fst[:, cols] = jnp.where(keep, result, 0.0).astype(BF)
        return 0

    lax.fori_loop(0, 4, last, 0)
    save(fst, layer_out)
    for g in SPECS:
        ag[g].finish()
    for copy in stores:
        copy.wait()
    for f in (6, 7):
        for copy in put_ab(f, f % 2):
            copy.wait()


def forward(length, tokens, first, shards, tables):
    rows, width = tokens.shape
    hidden = 8 * shards[GATE].shape[0]
    order = (QKV, OUT, GATE, UP, DOWN, GAIN)
    half = jax.ShapeDtypeStruct((rows, width), BF)
    pairs = half
    tall = jax.ShapeDtypeStruct((hidden, rows), BF)
    logs = jax.ShapeDtypeStruct((8, 2, rows), F32)
    wide = jax.ShapeDtypeStruct((rows, width), F32)
    fulls = [jax.ShapeDtypeStruct(full_shape(SPECS[g]), BF) for g in order]
    outs = [half, half, pairs, pairs, pairs, half, logs, wide, half, tall, tall, tall] + fulls
    anywhere = pl.BlockSpec(memory_space=pl.ANY)
    scratch = [pltpu.VMEM(s.shape, s.dtype) for s in fulls]
    scratch += [pltpu.VMEM(s.shape, s.dtype) for s in (half, half, half, pairs, pairs, pairs, half, logs, wide, half, tall)]
    scratch += [pltpu.VMEM((2, 2, hidden // 8, rows), BF)]
    scratch += [pltpu.VMEM((rows, 128), F32)] * 3
    scratch += [
        pltpu.SemaphoreType.DMA((6, 14)),
        pltpu.SemaphoreType.DMA((6, 14)),
        pltpu.SemaphoreType.DMA((6,)),
        pltpu.SemaphoreType.DMA((5,)),
        pltpu.SemaphoreType.DMA((len(outs),)),
        pltpu.SemaphoreType.DMA((2, 2)),
    ]
    return pl.pallas_call(
        forward_kernel,
        out_shape=outs,
        in_specs=[pl.BlockSpec(memory_space=pltpu.SMEM)] + [anywhere] * 11,
        out_specs=[anywhere] * len(outs),
        scratch_shapes=scratch,
        compiler_params=pltpu.CompilerParams(
            collective_id=0, has_side_effects=True, vmem_limit_bytes=63 << 20
        ),
        name="forward",
    )(length, tokens, first, *[shards[g] for g in order], *tables)


def rope_tables(rows):
    position = np.arange(rows, dtype=np.float32)[:, None]
    frequency = np.float32(10000.0) ** (-np.arange(32, dtype=np.float32) * np.float32(2.0) / np.float32(64))
    angle = (position * frequency[None, :]).astype(np.float32)
    cosine, sine, zero = np.cos(angle), np.sin(angle), np.zeros_like(angle)
    join = lambda parts: np.concatenate(parts, axis=1).astype(np.float32)
    return join([cosine] * 4), join([-sine, zero] * 2), join([zero, sine] * 2)


def aligned(index, multiple):
    return index if isinstance(index, int) else pl.multiple_of(index, multiple)


REDUCE = {g: SPECS[g][:2] for g in (DOWN, GATE, UP, OUT, QKV)}
REDUCE[GAIN] = (16, 128)
ORDER = (DOWN, GATE, UP, OUT, QKV, GAIN)


def buffers(g):
    rows, cols = REDUCE[g]
    half, kind = rows // 2, F32 if g == GAIN else BF
    shapes = [(2, 4, 2, rows, cols), (2, 4, half, cols), (4, 2, half, cols), (2, 4, half, cols), (3, 2, half, cols)]
    return [pltpu.VMEM(s, kind) for s in shapes] + [pltpu.VMEM((rows, cols), F32)]


class Scatter:
    def __init__(self, at, g, refs, send, recv, store, result):
        self.at, self.g, self.half = at, g, REDUCE[g][0] // 2
        self.r0, self.r1a, self.r1b, self.r2, self.r3, self.total = refs
        self.send, self.recv, self.store, self.result = send, recv, store, result
        self.copies = {}

    def copy(self, slot):
        source, target, peer = self.copies[slot]()
        return pltpu.make_async_remote_copy(
            src_ref=source,
            dst_ref=target,
            send_sem=self.send.at[self.g, slot],
            recv_sem=self.recv.at[self.g, slot],
            device_id=peer,
            device_id_type=MESH_ID,
        )

    def go(self, slot, ends):
        self.copies[slot] = ends
        self.copy(slot).start()

    def arrive(self, *slots):
        for slot in slots:
            self.copy(slot).wait_recv()

    def tick1(self):
        x, c, z, y = self.at
        low, high = pl.ds(0, self.half), pl.ds(self.half, self.half)
        self.go(0, lambda: (self.r0.at[:, :, 1 - y, low], self.r1a, device(x, c, z, 1 - y)))
        self.go(1, lambda: (self.r0.at[1 - x, :, :, high], self.r1b, device(1 - x, c, z, y)))

    def tick2(self):
        x, c, z, y = self.at
        low, high = pl.ds(0, self.half), pl.ds(self.half, self.half)
        self.arrive(0)

        def add_a(i, _):
            self.r1a[i // 4, i % 4] += self.r0[i // 4, i % 4, y, low]
            return 0

        def add_b(i, _):
            self.r1b[i // 2, i % 2] += self.r0[x, i // 2, i % 2, high]
            return 0

        lax.fori_loop(0, 8, add_a, 0)
        self.go(2, lambda: (self.r1a.at[1 - x], self.r2.at[0], device(1 - x, c, z, y)))
        self.arrive(1)
        lax.fori_loop(0, 8, add_b, 0)
        self.go(3, lambda: (self.r1b.at[:, 1 - y], self.r2.at[1], device(x, c, z, 1 - y)))

    def tick3(self):
        x, c, z, y = self.at
        self.arrive(2, 3)

        def add(i, _):
            self.r2[0, i] += self.r1a[x, i]
            self.r2[1, i] += self.r1b[i, y]
            return 0

        lax.fori_loop(0, 4, add, 0)
        for d in (1, 2, 3):
            to = lambda d=d: lax.rem(z + d, 4)
            self.go(3 + d, lambda d=d, to=to: (self.r2.at[:, to()], self.r3.at[d - 1], device(x, c, to(), y)))

    def tick4(self):
        x, c, z, y = self.at
        self.arrive(4, 5, 6)
        for part in range(2):
            total = self.r2[part, z].astype(F32)
            for d in range(3):
                total = total + self.r3[d, part].astype(F32)
            self.total[pl.ds(part * self.half, self.half)] = total
        self.out().start()

    def out(self):
        return pltpu.make_async_copy(self.total, self.result, self.store.at[self.g])

    def finish(self):
        for slot in self.copies:
            self.copy(slot).wait_send()
        self.out().wait()


def attend_back(q, k, v, do, o, lse, keep_dk, keep_dv, blk):
    rows = q.shape[0]
    k_turned = k.T
    products = (do.astype(F32) * o.astype(F32)).T
    key_index = lax.broadcasted_iota(jnp.int32, (blk, blk), 0)
    query_index = lax.broadcasted_iota(jnp.int32, (blk, blk), 1)
    allowed = key_index <= query_index
    out = []
    for j in reversed(range(rows // blk)):
        lo, hi = j * blk, (j + 1) * blk
        dq, probs, grads, queries, outs = [], [], [], [], []
        for head in range(2):
            mask = head_mask((blk, 128), head)
            qh = jnp.where(mask, q[lo:hi], 0)
            oh = jnp.where(mask, do[lo:hi], 0)
            delta = jnp.sum(products[head * 64 : head * 64 + 64, lo:hi], axis=0, keepdims=True)
            logs = lse[head][:, lo:hi]
            s = mm(k[:hi], qh, NT)
            dp = mm(v[:hi], oh, NT)
            p_tail = jnp.exp(jnp.where(allowed, s[lo:hi], -1000000000.0) - logs)
            ds = (p_tail * (dp[lo:hi] - delta)).astype(BF)
            p = p_tail.astype(BF)
            if j:
                p_head = jnp.exp(s[:lo] - logs)
                ds = jnp.concatenate([(p_head * (dp[:lo] - delta)).astype(BF), ds], axis=0)
                p = jnp.concatenate([p_head.astype(BF), p], axis=0)
            dq.append(mm(k_turned[head * 64 : head * 64 + 64, :hi], ds, NN))
            probs.append(p)
            grads.append(ds)
            queries.append(qh)
            outs.append(oh)
        dk = mm(jnp.concatenate(grads, axis=1), jnp.concatenate(queries, axis=0), NN)
        dv = mm(jnp.concatenate(probs, axis=1), jnp.concatenate(outs, axis=0), NN)
        if hi == rows:
            keep_dk[...] = dk
            keep_dv[...] = dv
        else:
            keep_dk[pl.ds(0, hi)] += dk
            keep_dv[pl.ds(0, hi)] += dv
        out.append(jnp.concatenate(dq, axis=0).T * 0.125)
    return jnp.concatenate(out[::-1], axis=0)


def backward_kernel(
    length, cot, tokens, n1, q, k, v, o, lse, x2, n2, h, a, b,
    g_qkv, g_out, g_gate, g_up, g_down, g_gain, cosine, low_sine, high_sine,
    input_grad, first_grad, red_down, red_gate, red_up, red_out, red_qkv, red_gain,
    *scratch,
):
    bufs = {g: scratch[6 * i : 6 * i + 6] for i, g in enumerate(ORDER)}
    (
        st_down, st_gate, st_up, st_qkv, st_gain, big, cf, cut, dx, gains,
        send, recv, send0, recv0, store, fetch, stream_sem, fg_sem,
    ) = scratch[36:]
    at = place()
    x, c, z, y = at
    other = device(x, 1 - c, z, y)
    rows, width = cot.shape
    hidden = h.shape[0]
    span = hidden // 8
    loads = {}

    def load(name, ends):
        index = len(loads)
        loads[name] = lambda: pltpu.make_async_copy(*ends(), fetch.at[index])
        loads[name]().start()

    load("cot", lambda: (cot, cf))
    load("h", lambda: (h, big.at[pl.ds(0, hidden)]))
    for own in range(2):
        for i in range(2):
            col = aligned((2 * i + (c if own else 1 - c)) * 256, 256)
            load(
    ("n2", own, i),
    lambda own=own, i=i, col=col: (n2.at[:, pl.ds(col, 256)], cut.at[own, :, pl.ds(i * 256, 256)]),
)
    load("gain", lambda: (g_gain.at[:, :, pl.ds(0, 32)], gains))
    greet(*at)
    reds = {DOWN: red_down, GATE: red_gate, UP: red_up, OUT: red_out, QKV: red_qkv, GAIN: red_gain}
    rs = {g: Scatter(at, g, bufs[g], send, recv, store, reds[g]) for g in ORDER}

    def swap(g, stage, slot, target, index):
        staged = stage.at[slot, :, :, pl.ds(0, 256)] if g == OUT else stage.at[slot]
        return pltpu.make_async_remote_copy(
            src_ref=staged,
            dst_ref=target,
            send_sem=send0.at[g, slot],
            recv_sem=recv0.at[g, index],
            device_id=other,
            device_id_type=MESH_ID,
        )

    def exchange(count, give, take, between=None):
        give(0)

        def body(i, _):
            give(i)
            take(i - 1)
            return 0

        edges = sorted({1, count} | set(between or {}))
        for lo, hi in zip(edges[:-1], edges[1:]):
            if between and lo in between:
                between[lo]()
            lax.fori_loop(lo, hi, body, 0)
        take(count - 1)

    def settled(copy, i):
        if isinstance(i, int):
            if i >= 2:
                copy(i - 2).wait_send()
            return

        @pl.when(i >= 2)
        def _():
            copy(i - 2).wait_send()

    live = length[0]
    loads["cot"]().wait()

    def mask_rows(i, _):
        at_rows = pl.ds(aligned(i * 256, 256), 256)
        keep = lax.broadcasted_iota(jnp.int32, (256, width), 0) + i * 256 < live
        cf[at_rows] = jnp.where(keep, cf[at_rows].astype(F32), 0.0).astype(BF)
        return 0

    lax.fori_loop(0, rows // 256, mask_rows, 0)
    loads["h"]().wait()
    r0 = bufs[DOWN][0]

    def down_copy(i):
        return swap(DOWN, st_down, i % 2, r0.at[i // 2, :, :, pl.ds(aligned((i % 2) * span, 16), span)], i)

    def down_part(i, core):
        f = 2 * (2 * (i // 2) + core) + i % 2
        return mm(big[pl.ds(aligned(f * span, 16), span)], cf[...], NN)

    def down_give(i):
        settled(down_copy, i)
        part = down_part(i, 1 - c)
        for fs in range(8):
            st_down[i % 2, fs // 2, fs % 2] = part[:, fs * 128 : fs * 128 + 128].astype(BF)
        down_copy(i).start()

    def down_take(i):
        part = down_part(i, c)
        down_copy(i).wait_recv()
        at_rows = pl.ds(aligned((i % 2) * span, 16), span)
        for fs in range(8):
            r0[i // 2, fs // 2, fs % 2, at_rows] += part[:, fs * 128 : fs * 128 + 128].astype(BF)

    exchange(4, lambda i: down_give(i), lambda i: down_take(i))
    rs[DOWN].tick1()

    def ffn(wd, ab):
        def stream(f, slot):
            at_f = pl.ds(aligned(f * span, 16), span)
            return [
                pltpu.make_async_copy(g_down.at[:, :, at_f], wd.at[slot], stream_sem.at[slot, 0]),
                pltpu.make_async_copy(a.at[at_f], ab.at[slot, 0], stream_sem.at[slot, 1]),
                pltpu.make_async_copy(b.at[at_f], ab.at[slot, 1], stream_sem.at[slot, 2]),
            ]

        for copy in stream(0, 0):
            copy.start()
        for name in list(loads):
            if name[0] == "n2":
                loads[name]().wait()

        def pair_copy(g, stage):
            return lambda f: swap(g, stage, f % 2, bufs[g][0].at[:, f // 2, f % 2], f)

        up_copy, gate_copy = pair_copy(UP, st_up), pair_copy(GATE, st_gate)

        def give(f):
            slot = f % 2

            def ahead():
                for copy in stream(f + 1, 1 - slot):
                    copy.start()

            if isinstance(f, int):
                ahead()
            else:
                pl.when(f < 7)(ahead)

            for copy in stream(f, slot):
                copy.wait()
            weights = jnp.concatenate([wd[slot, i // 2, i % 2] for i in range(8)], axis=1)
            dh = mm(weights, cf[...], NT)
            dgate = (dh * ab[slot, 0].astype(F32)).astype(BF)
            dup = (dh * ab[slot, 1].astype(F32)).astype(BF)
            at_f = aligned(f * span, 16)
            big[pl.ds(at_f, span)] = dgate
            big[pl.ds(hidden + at_f, span)] = dup
            for grad, stage, copy in ((dgate, st_gate, gate_copy), (dup, st_up, up_copy)):
                settled(copy, f)
                part = mm(grad, cut[0], NN).astype(BF)
                stage[slot, 0] = part[:, 0:256]
                stage[slot, 1] = part[:, 256:512]
                copy(f).start()

        def take(f):
            at_f = aligned(f * span, 16)
            for g, start, copy in ((GATE, 0, gate_copy), (UP, hidden, up_copy)):
                part = mm(big[pl.ds(start + at_f, span)], cut[1], NN).astype(BF)
                copy(f).wait_recv()
                into = bufs[g][0]
                into[0, f // 2, f % 2] += part[:, 0:256]
                into[1, f // 2, f % 2] += part[:, 256:512]

        exchange(
            8,
            lambda f: give(f),
            lambda f: take(f),
            {6: rs[DOWN].tick2},
        )
        for f in (6, 7):
            up_copy(f).wait_send()
            gate_copy(f).wait_send()
        for i in (2, 3):
            down_copy(i).wait_send()

    pl.run_scoped(ffn, pltpu.VMEM((2, 4, 2, span, 128), BF), pltpu.VMEM((2, 2, span, rows), BF))
    rs[GATE].tick1()
    rs[UP].tick1()
    rs[DOWN].tick3()

    def dn2(weights):
        def stream(i, slot):
            cols = pl.ds(aligned(i * 256, 256), 256)
            return [
                pltpu.make_async_copy(
                    w.at[f // 2, f % 2, :, cols], weights.at[slot, n, pl.ds(f * span, span)], stream_sem.at[slot, 3 + n * 8 + f]
                )
                for n, w in enumerate((g_gate, g_up))
                for f in range(8)
            ]

        for copy in stream(0, 0):
            copy.start()

        def body(i, _):
            slot = i % 2

            @pl.when(i < 3)
            def _():
                for copy in stream(i + 1, 1 - slot):
                    copy.start()

            for copy in stream(i, slot):
                copy.wait()
            cols = pl.ds(aligned(i * 256, 256), 256)
            dx[:, cols] = mm(big[pl.ds(0, hidden)], weights[slot, 0], TN) + mm(
                big[pl.ds(hidden, hidden)], weights[slot, 1], TN
            )
            return 0

        lax.fori_loop(0, 4, body, 0)

    pl.run_scoped(dn2, pltpu.VMEM((2, 2, hidden, 256), BF))
    for i, (name, source) in enumerate((("q", q), ("k", k), ("v", v))):
        load(name, lambda source=source, i=i: (source, big.at[pl.ds(i * rows, rows)]))
    rs[GATE].tick2()
    rs[DOWN].tick4()
    loads["gain"]().wait()
    gain = jnp.concatenate([gains[i // 2, i % 2] for i in range(8)], axis=1).astype(F32)
    gain_one, gain_two = gain[0:1], gain[16:17]

    def norm_back(u, dy, gain):
        inverse = lax.rsqrt(jnp.mean(u * u, axis=-1, keepdims=True) + 1e-06)
        scaled = dy * gain
        along = jnp.sum(scaled * u, axis=-1, keepdims=True) * (inverse * inverse * inverse / width)
        return scaled * inverse - u * along, jnp.sum(dy * u * inverse, axis=0, keepdims=True)

    def mid(wide):
        copy = pltpu.make_async_copy(x2, wide, stream_sem.at[0, 0])
        copy.start()
        copy.wait()

        def body(i, total):
            at_rows = pl.ds(aligned(i * 128, 128), 128)
            grad, gain_part = norm_back(wide[at_rows], dx[at_rows], gain_two)
            grad = grad + cf[at_rows].astype(F32)
            dx[at_rows] = grad
            big[pl.ds(aligned(3 * rows + i * 128, 128), 128)] = grad.astype(BF)
            return total + gain_part

        return lax.fori_loop(0, rows // 128, body, jnp.zeros((1, width), F32))

    gain_two_sum = pl.run_scoped(mid, pltpu.VMEM((rows, width), F32))
    rs[UP].tick2()

    def attention(ov, fg, cos, sin_lo, sin_hi, logs, dk_sum, dv_sum):
        load("o", lambda: (o, ov))
        load("lse", lambda: (lse, logs))
        load("cos", lambda: (cosine, cos))
        load("lo", lambda: (low_sine, sin_lo))
        load("hi", lambda: (high_sine, sin_hi))
        do = cf

        def heads_back(wo):
            copy = pltpu.make_async_copy(g_out, wo, stream_sem.at[0, 0])
            copy.start()
            loads["o"]().wait()
            copy.wait()

            def body(i, _):
                at_rows = pl.ds(aligned(i * 256, 256), 256)
                weights = jnp.concatenate([wo[f // 2, f % 2, at_rows] for f in range(8)], axis=1)
                do[:, at_rows] = mm(big[pl.ds(3 * rows, rows)], weights, NT).astype(BF)
                return 0

            lax.fori_loop(0, 4, body, 0)

        pl.run_scoped(heads_back, pltpu.VMEM((4, 2, width, 128), BF))
        r0_out = bufs[OUT][0]

        def out_copy(i):
            return swap(OUT, st_down, i % 2, r0_out.at[i], i)

        def out_part(i, core):
            col = pl.ds(aligned((2 * i + core) * 256, 256), 256)
            return mm(ov[:, col], big[pl.ds(3 * rows, rows)], TN)

        def out_give(i):
            part = out_part(i, 1 - c)
            for fs in range(8):
                st_down[i % 2, fs // 2, fs % 2, 0:256] = part[:, fs * 128 : fs * 128 + 128].astype(BF)
            out_copy(i).start()

        def out_take(i):
            part = out_part(i, c)
            out_copy(i).wait_recv()
            for fs in range(8):
                r0_out[i, fs // 2, fs % 2] += part[:, fs * 128 : fs * 128 + 128].astype(BF)

        exchange(2, lambda i: out_give(i), lambda i: out_take(i))
        rs[OUT].tick1()
        rs[GATE].tick3()
        for own in range(2):
            for i in range(2):
                col = aligned((2 * i + (c if own else 1 - c)) * 256, 256)
                load(
    ("n1", own, i),
    lambda own=own, i=i, col=col: (n1.at[:, pl.ds(col, 256)], cut.at[own, :, pl.ds(i * 256, 256)]),
)
        for name in ("q", "k", "v", "lse", "cos", "lo", "hi"):
            loads[name]().wait()

        def fg_copy(p):
            cols = pl.ds(aligned(p * 128, 128), 128)
            return pltpu.make_async_copy(fg.at[p % 2], first_grad.at[:, cols], fg_sem.at[p % 2])

        def pair(p, _):
            cols = pl.ds(aligned(p * 128, 128), 128)
            dq = attend_back(
                big[pl.ds(0, rows), cols], big[pl.ds(rows, rows), cols], big[pl.ds(2 * rows, rows), cols],
                do[:, cols], ov[:, cols], [logs[p, pl.ds(i, 1)] for i in range(2)], dk_sum, dv_sum, min(256, rows),
            )

            @pl.when(p >= 2)
            def _():
                fg_copy(p - 2).wait()

            big[pl.ds(0, rows), cols] = turn(dq, cos[...], -sin_lo[...], -sin_hi[...]).astype(BF)
            big[pl.ds(rows, rows), cols] = turn(dk_sum[...], cos[...], -sin_lo[...], -sin_hi[...]).astype(BF)
            half = 0.5 * dv_sum[...]
            fg[p % 2] = half
            fg_copy(p).start()
            big[pl.ds(2 * rows, rows), cols] = half.astype(BF)
            return 0

        lax.fori_loop(0, 2, pair, 0)
        rs[UP].tick3()
        rs[GATE].tick4()
        lax.fori_loop(2, 4, pair, 0)
        rs[OUT].tick2()
        rs[UP].tick4()
        lax.fori_loop(4, 6, pair, 0)
        rs[OUT].tick3()
        lax.fori_loop(6, 8, pair, 0)
        rs[OUT].tick4()
        for name in list(loads):
            if name[0] == "n1":
                loads[name]().wait()
        for part in range(3):
            for i in range(8):
                load(
                    ("w", part, i),
                    lambda part=part, i=i: (
                        g_qkv.at[i // 2, i % 2, :, pl.ds(part * 128, 128)],
                        (cf.at[:] if part == 2 else big.at[pl.ds((3 + part) * rows, rows)]).at[:, pl.ds(i * 128, 128)],
                    ),
                )
        r0_qkv = bufs[QKV][0]

        def qkv_copy(i):
            return swap(QKV, st_qkv, i % 2, r0_qkv.at[:, i], i)

        def qkv_parts(i, own):
            cols = pl.ds(aligned(i * 256, 256), 256)
            sources = [big[pl.ds(n * rows, rows), cols] for n in range(3)]
            return [mm(cut[own], source, TN).astype(BF) for source in sources]

        def qkv_give(i):
            settled(qkv_copy, i)
            for n, part in enumerate(qkv_parts(i, 0)):
                for xx in range(2):
                    for yy in range(2):
                        st_qkv[i % 2, xx, yy, :, pl.ds(n * 128, 128)] = part[
                            xx * 256 : xx * 256 + 256, yy * 128 : yy * 128 + 128
                        ]
            qkv_copy(i).start()

        def qkv_take(i):
            parts = qkv_parts(i, 1)
            qkv_copy(i).wait_recv()
            for n, part in enumerate(parts):
                for xx in range(2):
                    for yy in range(2):
                        r0_qkv[xx, i, yy, :, pl.ds(n * 128, 128)] += part[
                            xx * 256 : xx * 256 + 256, yy * 128 : yy * 128 + 128
                        ]

        exchange(4, lambda i: qkv_give(i), lambda i: qkv_take(i))
        rs[QKV].tick1()
        load("tok", lambda: (tokens, ov))
        for name in list(loads):
            if name[0] == "w":
                loads[name]().wait()

        def finish_norm(dn):
            def body(i, _):
                at_rows = pl.ds(aligned(i * 256, 256), 256)
                dn[:, at_rows] = (
                    mm(big[pl.ds(0, rows)], big[pl.ds(aligned(3 * rows + i * 256, 256), 256)], NT)
                    + mm(big[pl.ds(rows, rows)], big[pl.ds(aligned(4 * rows + i * 256, 256), 256)], NT)
                    + mm(big[pl.ds(2 * rows, rows)], cf[at_rows], NT)
                )
                return 0

            lax.fori_loop(0, 4, body, 0)
            rs[QKV].tick2()
            loads["tok"]().wait()

            def body(i, total):
                at_rows = pl.ds(aligned(i * 128, 128), 128)
                grad, gain_part = norm_back(ov[at_rows].astype(F32), dn[at_rows], gain_one)
                dx[at_rows] = dx[at_rows] + grad
                return total + gain_part

            return lax.fori_loop(0, rows // 128, body, jnp.zeros((1, width), F32))

        total = pl.run_scoped(finish_norm, pltpu.VMEM((rows, width), F32))
        for p in (6, 7):
            fg_copy(p).wait()
        return total

    half = pltpu.VMEM((rows, width), BF)
    slim = pltpu.VMEM((rows, 128), F32)
    gain_one_sum = pl.run_scoped(
        attention, half, pltpu.VMEM((2, rows, 128), F32), slim, slim, slim, pltpu.VMEM(lse.shape, F32), slim, slim
    )
    grad_copy = pltpu.make_async_copy(dx, input_grad, fetch.at[len(loads)])
    grad_copy.start()
    for i in range(8):
        cols = slice(i * 128, i * 128 + 128)
        st_gain[0, i // 2, i % 2, 0:8] = jnp.broadcast_to(gain_one_sum[:, cols], (8, 128))
        st_gain[0, i // 2, i % 2, 8:16] = jnp.broadcast_to(gain_two_sum[:, cols], (8, 128))
    st_gain[1] = st_gain[0]
    r0_gain = bufs[GAIN][0]
    swaps = [swap(GAIN, st_gain, i, r0_gain.at[i], i) for i in range(2)]
    for copy in swaps:
        copy.start()
    for i, copy in enumerate(swaps):
        copy.wait_recv()
        r0_gain[i] += st_gain[i]
    rs[GAIN].tick1()
    rs[GAIN].tick2()
    rs[QKV].tick3()
    rs[GAIN].tick3()
    rs[GAIN].tick4()
    rs[QKV].tick4()
    for copy in swaps:
        copy.wait_send()
    for i in (0, 1):
        swap(OUT, st_down, i, bufs[OUT][0].at[i], i).wait_send()
        swap(QKV, st_qkv, i, bufs[QKV][0].at[:, 2 + i], 2 + i).wait_send()
    for g in ORDER:
        rs[g].finish()
    grad_copy.wait()


def backward(length, cot, tokens, saved, tables):
    rows, width = tokens.shape
    hidden = saved[8].shape[0]
    outs = [jax.ShapeDtypeStruct((rows, width), F32)] * 2
    outs += [jax.ShapeDtypeStruct(REDUCE[g], F32) for g in ORDER]
    anywhere = pl.BlockSpec(memory_space=pl.ANY)
    scratch = [buffer for g in ORDER for buffer in buffers(g)]
    scratch += [
        pltpu.VMEM((2, 4, 2, hidden // 8, 128), BF),
        pltpu.VMEM((2, 2, hidden // 8, 256), BF),
        pltpu.VMEM((2, 2, hidden // 8, 256), BF),
        pltpu.VMEM((2, 2, 2, 256, 384), BF),
        pltpu.VMEM((2, 4, 2, 16, 128), F32),
        pltpu.VMEM((2 * hidden, width), BF),
        pltpu.VMEM((rows, width), BF),
        pltpu.VMEM((2, rows, 512), BF),
        pltpu.VMEM((rows, width), F32),
        pltpu.VMEM((4, 2, 32, 128), BF),
        pltpu.SemaphoreType.DMA((6, 7)),
        pltpu.SemaphoreType.DMA((6, 7)),
        pltpu.SemaphoreType.DMA((6, 2)),
        pltpu.SemaphoreType.DMA((6, 8)),
        pltpu.SemaphoreType.DMA((6,)),
        pltpu.SemaphoreType.DMA((64,)),
        pltpu.SemaphoreType.DMA((2, 19)),
        pltpu.SemaphoreType.DMA((2,)),
    ]
    return pl.pallas_call(
        backward_kernel,
        out_shape=outs,
        in_specs=[pl.BlockSpec(memory_space=pltpu.SMEM)] + [anywhere] * (2 + len(saved) + 3),
        out_specs=[anywhere] * len(outs),
        scratch_shapes=scratch,
        compiler_params=pltpu.CompilerParams(
            collective_id=1, has_side_effects=True, vmem_limit_bytes=63 << 20
        ),
        name="backward",
    )(length, cot, tokens, *saved, *tables)


def on_slice(
    tokens, first_values, lengths, cotangent, w_query, w_key, w_value, w_out, w_gate, w_up, w_down, norm_one, norm_two,
):
    rows, width = tokens.shape
    gains = jnp.concatenate([jnp.broadcast_to(g[None], (16, 128)) for g in (norm_one, norm_two)], axis=0)
    shards = {
        QKV: jnp.concatenate([w_query, w_key, w_value], axis=1),
        OUT: w_out,
        GATE: w_gate.T,
        UP: w_up.T,
        DOWN: w_down,
        GAIN: gains,
    }
    tables = [jnp.asarray(t) for t in rope_tables(rows)]
    layer_out, *saved = forward(lengths, tokens, first_values, shards, tables)
    input_grad, first_grad, down, gate, up, out, qkv, gain = backward(lengths, cotangent, tokens, saved, tables)
    return (
        layer_out, input_grad, first_grad, qkv[:, 0:128], qkv[:, 128:256], qkv[:, 256:384], out, gate.T, up.T, down,
        gain[0], gain[8],
    )


def solution(mesh):
    in_specs = (
        P(("dp", "fsdp"), None),
        P(("dp", "fsdp"), None),
        P(("dp", "fsdp")),
        P(("dp", "fsdp"), None),
        P("dp", "fsdp"),
        P("dp", "fsdp"),
        P("dp", "fsdp"),
        P("dp", "fsdp"),
        P("dp", "fsdp"),
        P("dp", "fsdp"),
        P("dp", "fsdp"),
        P("fsdp"),
        P("fsdp"),
    )
    out_specs = (
        P(("dp", "fsdp"), None),
        P(("dp", "fsdp"), None),
        P(("dp", "fsdp"), None),
        P("dp", "fsdp"),
        P("dp", "fsdp"),
        P("dp", "fsdp"),
        P("dp", "fsdp"),
        P("dp", "fsdp"),
        P("dp", "fsdp"),
        P("dp", "fsdp"),
        P("fsdp"),
        P("fsdp"),
    )
    on_device = on_slice if dict(mesh.shape) == {"dp": 4, "fsdp": 8} else on_device_general
    return jax.shard_map(
        on_device, mesh=mesh, in_specs=in_specs, out_specs=out_specs, check_vma=False
    )
```
